128 devices in a mesh: gx: 4 (over y), gy: 32 (over z, x, core).
Axes of the slice: x: 4, y: 4, z: 4, core: 2. Of those that a mesh axis runs over, the one named last changes fastest.
Arguments:
- fields: float32 [10, 64, 2048, 128], P(None, 'gx', 'gy'), may hold values from -6 to 6
- diffusivity: float32 [10], replicated, may hold values from 0.03 to 0.12
- decay_rates: float32 [10], replicated, may hold values from 0.3 to 1
- reaction_matrix: float32 [10, 10], replicated, may hold values from -1 to 1
- owner_index: int32 [4, 32768, 1], P('gx', 'gy'), may hold values from 0 to 31, as said below
- flame_flag: int32 [4, 32768, 1], P('gx', 'gy'), may hold values from 0 to 1, as said below
Outputs:
- new_fields: float32 [10, 64, 2048, 128], P(None, 'gx', 'gy')
- owner_heat: float32 [4, 32], P('gx', 'gy')
The draws below stay inside these ranges and needn't reach their ends.
Inputs may be any that keep to these rules, and one draw needn't show every extreme that they name: `flame_flag`: each device holds exactly 256 or 32 flame blocks; in each index of gx exactly 4 devices along gy, consecutive with wraparound from a drawn start, hold 256. `owner_index`: the flame blocks of one index of gx, taken in order of device and then block, are dealt to owners in turn from a drawn first owner; so one device names each owner for at most 8 of its flame blocks and each owner receives at most 60 flame blocks, both bounds reached on every draw; a block outside the flame names its own device's index along gy.
All inputs are finite; a program needn't handle non-finite values.
Results may differ from the reference program's by a relative error of at most 0.0003.
Values sent between devices are 32-bit elements; how exact they have to be, the bound alone decides.
A program may use at most 128 MiB of HBM per device.

```python
import math
import jax
import jax.numpy as jnp
from jax import lax

COMP = 10
CX = 16
CY = 64
CZ = 128
SWEEPS = 2
COOL_SUB = 1
FLAME_SUB = 10
NEWTON = 3
CH = 1024
FMAX = 256
FLOW = 32
NB = 4
FTOT = 1920
RMAX = 60
NX = 64
NY = 2048
N_GX = 4
N_GY = 32


def flame_layout(key):
    starts = jax.random.randint(jax.random.fold_in(key, 11), (N_GX,), 0, N_GY)
    shifts = jax.random.randint(jax.random.fold_in(key, 12), (N_GX,), 0, N_GY)
    devices_y = jnp.arange(N_GY, dtype=jnp.int32)
    in_band = (devices_y[None, :] - starts[:, None]) % N_GY < NB
    counts = jnp.where(in_band, FMAX, FLOW).astype(jnp.int32)

    def one_device(number):
        return jax.random.permutation(jax.random.fold_in(key, 100 + number), CH).astype(jnp.int32)
    orders = jax.vmap(one_device)(jnp.arange(N_GX * N_GY, dtype=jnp.int32)).reshape(N_GX, N_GY, CH)
    flags = (orders < counts[:, :, None]).astype(jnp.int32).reshape(N_GX, N_GY * CH)
    rank = jnp.cumsum(flags, axis=1) - flags
    home = jnp.repeat(devices_y, CH)[None, :]
    owners = jnp.where(flags == 1, (rank + shifts[:, None]) % N_GY, home).astype(jnp.int32)
    return (flags, owners)


def draw_flame_flag(key, part):
    layout = flame_layout(key)
    return layout[0][:, :, None]


def draw_owner_index(key, part):
    layout = flame_layout(key)
    return layout[1][:, :, None]


def levels(rng, extent, cuts, smallest, high):
    level = 1.0
    for dim, blocks in cuts:
        draws = jax.random.uniform(jax.random.fold_in(jax.random.fold_in(rng, 6), dim), (blocks,), jnp.float32, smallest / len(cuts), high / len(cuts))
        level = level * jnp.repeat(jnp.exp(draws), extent[dim] // blocks).reshape((-1,) + (1,) * (len(extent) - 1 - dim))
    return level


def normal_values(rng, dims, width, most, shards=(), kind=jnp.bfloat16):
    loudness = levels(rng, dims, shards, -0.22, 0.18) if shards else 1.0
    entries = jax.random.normal(rng, dims, jnp.float32) * width * loudness
    return jnp.minimum(jnp.maximum(entries, -most), most).astype(kind)


def setup_inputs(seed: int = 0) -> dict:
    arg_keys = jax.random.split(jax.random.key(seed), 7)
    return {
        "fields": normal_values(arg_keys[0], (COMP, NX, NY, CZ), 1.0, 6.0, ((1, 4), (2, 32)), jnp.float32),
        "diffusivity": jnp.clip(jnp.exp(jax.random.uniform(arg_keys[1], (COMP,), jnp.float32, math.log(0.03), math.log(0.12))), 0.03, 0.12),
        "decay_rates": jnp.clip(jnp.exp(jax.random.uniform(arg_keys[2], (COMP,), jnp.float32, math.log(0.3), math.log(1.0))), 0.3, 1.0),
        "reaction_matrix": normal_values(arg_keys[3], (COMP, COMP), (4 * COMP) ** -0.5, 1.0, (), jnp.float32),
        "owner_index": draw_owner_index(jax.random.fold_in(arg_keys[6], 71), 0),
        "flame_flag": draw_flame_flag(jax.random.fold_in(arg_keys[6], 71), 0),
    }


H_STEP = 0.2

def diffuse(fields, diffusivity):
    padded = jnp.pad(fields, ((0, 0), (1, 1), (1, 1), (1, 1)))
    center = padded[:, 1:-1, 1:-1, 1:-1]
    laplace = padded[:, 2:, 1:-1, 1:-1] + padded[:, :-2, 1:-1, 1:-1]
    laplace = laplace + padded[:, 1:-1, 2:, 1:-1] + padded[:, 1:-1, :-2, 1:-1]
    laplace = laplace + padded[:, 1:-1, 1:-1, 2:] + padded[:, 1:-1, 1:-1, :-2] - 6.0 * center
    return center + diffusivity[:, None, None, None] * laplace

def react(blocks, reaction_matrix, decay_rates, count):
    divisor = 1.0 + H_STEP * decay_rates[:, None]
    current = blocks
    for substep in range(count):
        anchor = current
        for newton in range(NEWTON):
            gating = jax.nn.sigmoid(current[..., -1:, :])
            mixing = jnp.einsum('ij,...jn->...in', reaction_matrix, current, precision=lax.Precision.HIGHEST)
            current = (anchor + H_STEP * gating * mixing) / divisor
    return current

def reference(fields, diffusivity, decay_rates, reaction_matrix, owner_index, flame_flag):
    for sweep_count in range(SWEEPS):
        fields = diffuse(fields, diffusivity)
    columns = fields.reshape(COMP, N_GX, CX, N_GY, CY, CZ).transpose(1, 3, 2, 4, 0, 5).reshape(N_GX, N_GY * CH, COMP, CZ)
    cool = react(columns, reaction_matrix, decay_rates, COOL_SUB)

    def one_row(pieces):
        flag_row, column_row, cool_row, owner_row = pieces
        where = jnp.nonzero(flag_row, size=FTOT)[0].astype(jnp.int32)
        picked = column_row[where]
        hot = react(picked, reaction_matrix, decay_rates, FLAME_SUB)
        merged = cool_row.at[where].set(hot)
        gain = lax.optimization_barrier(jnp.sum(hot[:, -1, :] - picked[:, -1, :], axis=-1)) / math.sqrt(CZ)
        onehot = (owner_row[where][:, None] == jnp.arange(N_GY, dtype=jnp.int32)[None, :]).astype(jnp.float32)
        heat = jnp.einsum('c,cj->j', gain, onehot, precision=lax.Precision.HIGHEST) / math.sqrt(RMAX)
        return (merged, heat)
    merged, owner_heat = lax.map(one_row, (flame_flag[:, :, 0], columns, cool, owner_index[:, :, 0]))
    new_fields = merged.reshape(N_GX, N_GY, CX, CY, COMP, CZ).transpose(4, 0, 2, 1, 3, 5).reshape(COMP, NX, NY, CZ)
    return (new_fields, owner_heat)
```

```python
import functools
import math

import jax
import jax.numpy as jnp
from jax import lax
from jax.experimental import pallas as pl
from jax.experimental.pallas import tpu as pltpu
from jax.sharding import PartitionSpec as P

H_STEP = 0.2
FLAME_SUB = 10
COMP = 10
CX, CY, CZ = 16, 64, 128
CH = CX * CY
FMAX = 256
RMAX = 60

F32, BF16 = jnp.float32, jnp.bfloat16
MESH = pl.DeviceIdType.MESH
VMEM = pl.BlockSpec(memory_space=pltpu.VMEM)
SMEM = pl.BlockSpec(memory_space=pltpu.SMEM)
ANY = pl.BlockSpec(memory_space=pl.ANY)
LIMIT = 56 << 20


def split(values):
    high = values.astype(BF16)
    low = (values - high.astype(F32)).astype(BF16)
    return high, low


def halo_kernel(n_gx, n_gy, fields, taps, diff, out, ext, mid, res, in_sem, send, recv, out_sem):
    gx, gy = lax.axis_index("gx"), lax.axis_index("gy")
    xm, xp = lax.rem(gx + n_gx - 1, n_gx), lax.rem(gx + 1, n_gx)
    ym, yp = lax.rem(gy + n_gy - 1, n_gy), lax.rem(gy + 1, n_gy)
    load = pltpu.make_async_copy(fields, ext.at[:, pl.ds(2, CX), pl.ds(8, CY), :], in_sem)
    load.start()
    targets = [
        (xp, gy), (xm, gy), (gx, yp), (gx, ym), (xp, yp), (xp, ym), (xm, yp), (xm, ym),
    ]
    barrier = pltpu.get_barrier_semaphore()
    for target in targets:
        pl.semaphore_signal(barrier, inc=1, device_id=target, device_id_type=MESH)
    pl.semaphore_wait(barrier, 8)
    ranges = [
        ((CX - 2, 2), (0, CY), (0, 8)),
        ((0, 2), (0, CY), (CX + 2, 8)),
        ((0, CX), (CY - 8, 8), (2, 0)),
        ((0, CX), (0, 8), (2, CY + 8)),
        ((CX - 1, 1), (CY - 8, 8), (1, 0)),
        ((CX - 1, 1), (0, 8), (1, CY + 8)),
        ((0, 1), (CY - 8, 8), (CX + 2, 0)),
        ((0, 1), (0, 8), (CX + 2, CY + 8)),
    ]
    copies = []
    for number, (target, (xs, ys, (dx, dy))) in enumerate(zip(targets, ranges)):
        copies.append(
            pltpu.make_async_remote_copy(
                src_ref=fields.at[:, pl.ds(*xs), pl.ds(*ys), :],
                dst_ref=ext.at[:, pl.ds(dx, xs[1]), pl.ds(dy, ys[1]), :],
                send_sem=send.at[number],
                recv_sem=recv.at[number],
                device_id=target,
                device_id_type=MESH,
            )
        )
    for number in (0, 1, 2, 3, 4, 5, 6, 7):
        copies[number].start()
    load.wait()

    def first(c, x, count):
        d = diff[c]
        shape = (count * 80, CZ)
        v = ext[c, pl.ds(x, count)].reshape(shape)
        near = ext[c, pl.ds(x - 1, count)].reshape(shape) + ext[c, pl.ds(x + 1, count)].reshape(shape)
        near = near + pltpu.roll(v, 1, 0) + pltpu.roll(v, shape[0] - 1, 0)
        near = near + jnp.dot(
            jnp.concatenate(split(v), axis=1), taps[...], preferred_element_type=F32
        )
        mid[c, pl.ds(x - 1, count)] = (v + d * near).reshape(count, 80, CZ)

    def second(c, x, count):
        d = diff[c]
        shape = (count * 80, CZ)
        v = mid[c, pl.ds(x + 1, count)].reshape(shape)
        near = mid[c, pl.ds(x, count)].reshape(shape) + mid[c, pl.ds(x + 2, count)].reshape(shape)
        near = near + pltpu.roll(v, 1, 0) + pltpu.roll(v, shape[0] - 1, 0)
        near = near + jnp.dot(
            jnp.concatenate(split(v), axis=1), taps[...], preferred_element_type=F32
        )
        res[c, pl.ds(x, count)] = (v + d * near).reshape(count, 80, CZ)[:, 8 : 8 + CY]

    def clear(ref, xs, ys):
        @pl.loop(0, COMP)
        def _(c):
            ref[c, pl.ds(*xs), pl.ds(*ys), :] = jnp.zeros((xs[1], ys[1], CZ), F32)

    def edges(ref, xs):
        @pl.when(gy == 0)
        def _():
            clear(ref, xs, (0, 8))

        @pl.when(gy == n_gy - 1)
        def _():
            clear(ref, xs, (CY + 8, 8))

    copies[2].wait_recv()
    copies[3].wait_recv()
    edges(ext, (2, CX))

    @pl.loop(0, COMP)
    def _(c):
        first(c, 3, 7)
        first(c, 10, 7)

    edges(mid, (2, CX - 2))

    @pl.loop(0, COMP)
    def _(c):
        second(c, 2, 6)
        second(c, 8, 6)
        pltpu.make_async_copy(
            res.at[c, pl.ds(2, CX - 4)], out.at[c, pl.ds(2, CX - 4)], out_sem.at[c]
        ).start()

    for number in (0, 1, 4, 5, 6, 7):
        copies[number].wait_recv()
    edges(ext, (1, 1))
    edges(ext, (CX + 2, 1))

    @pl.when(gx == 0)
    def _():
        clear(ext, (0, 2), (0, CY + 16))

    @pl.when(gx == n_gx - 1)
    def _():
        clear(ext, (CX + 2, 2), (0, CY + 16))

    @pl.loop(0, COMP)
    def _(c):
        first(c, 1, 2)
        first(c, CX + 1, 2)

    edges(mid, (1, 1))
    edges(mid, (CX, 1))

    @pl.when(gx == 0)
    def _():
        clear(mid, (0, 1), (0, CY + 16))

    @pl.when(gx == n_gx - 1)
    def _():
        clear(mid, (CX + 1, 1), (0, CY + 16))

    @pl.loop(0, COMP)
    def _(c):
        second(c, 0, 2)
        second(c, CX - 2, 2)
        pltpu.make_async_copy(
            res.at[c, pl.ds(0, 2)], out.at[c, pl.ds(0, 2)], out_sem.at[COMP + c]
        ).start()
        pltpu.make_async_copy(
            res.at[c, pl.ds(CX - 2, 2)], out.at[c, pl.ds(CX - 2, 2)], out_sem.at[2 * COMP + c]
        ).start()

    for copy in copies:
        copy.wait_send()

    @pl.loop(0, COMP)
    def _(c):
        pltpu.make_async_copy(
            res.at[c, pl.ds(2, CX - 4)], out.at[c, pl.ds(2, CX - 4)], out_sem.at[c]
        ).wait()
        pltpu.make_async_copy(
            res.at[c, pl.ds(0, 2)], out.at[c, pl.ds(0, 2)], out_sem.at[COMP + c]
        ).wait()
        pltpu.make_async_copy(
            res.at[c, pl.ds(CX - 2, 2)], out.at[c, pl.ds(CX - 2, 2)], out_sem.at[2 * COMP + c]
        ).wait()


def sigmoid(x):
    return 0.5 * jnp.tanh(0.5 * x) + 0.5


def substep(state, matrix, inverse):
    high, low = split(state)
    r = jnp.dot(matrix, jnp.concatenate([high, low, high], axis=0), preferred_element_type=F32)
    last = state[72:80]
    base = last * inverse[72:80]
    g0 = sigmoid(last)
    g1 = sigmoid(base + g0 * r[240:248])
    g2 = sigmoid(base + g1 * (r[72:80] + g0 * r[248:256]))
    rows = []
    for c in range(COMP):
        at = 8 * c
        inner = r[80 + at : 88 + at] + g0 * r[160 + at : 168 + at]
        rows.append(state[at : at + 8] * inverse[at : at + 8] + g2 * (r[at : at + 8] + g1 * inner))
    return rows


CHUNK = 128


def chem_kernel(u2, matrix, inverse, index, count, owners, out, terms, uv, ov, cur, start_t, in_sem, out_sem):
    for k in range(CH // CHUNK):
        pltpu.make_async_copy(
            u2.at[:, pl.ds(k * CHUNK, CHUNK), :], uv.at[:, pl.ds(k * CHUNK, CHUNK), :], in_sem.at[k]
        ).start()
    inv = inverse[...]
    inv = jnp.concatenate([inv, inv], axis=1)

    @pl.loop(0, CH // CHUNK)
    def _(k):
        part = pl.ds(pl.multiple_of(k * CHUNK, CHUNK), CHUNK)
        pltpu.make_async_copy(u2.at[:, part, :], uv.at[:, part, :], in_sem.at[k]).wait()
        for t in range(CHUNK // 16):
            def group(w):
                at = pl.multiple_of(k * CHUNK + t * 16 + w * 8, 8)
                return jnp.concatenate([uv[c, pl.ds(at, 8), :] for c in range(COMP)], axis=0)

            rows = substep(jnp.concatenate([group(0), group(1)], axis=1), matrix[...], inv)
            for w in range(2):
                at = pl.multiple_of(k * CHUNK + t * 16 + w * 8, 8)
                for c in range(COMP):
                    ov[c, pl.ds(at, 8), :] = rows[c][:, w * CZ : (w + 1) * CZ]

    @pl.loop(0, FMAX // 8)
    def _(g):
        for r in range(8):
            at = index[g * 8 + r]
            for c in range(COMP):
                cur[g, pl.ds(c * 8 + r, 1), :] = uv[c, pl.ds(at, 1), :]
        start_t[g] = cur[g, 72:80, :]

    @pl.loop(0, FLAME_SUB)
    def _(s):
        for t in range(FMAX // 16):
            rows = substep(
                jnp.concatenate([cur[2 * t], cur[2 * t + 1]], axis=1), matrix[...], inv
            )
            new = jnp.concatenate(rows, axis=0)
            cur[2 * t] = new[:, :CZ]
            cur[2 * t + 1] = new[:, CZ:]

    gain = (cur[:, 72:80, :] - start_t[...]).reshape(FMAX, CZ)
    onehot = (lax.broadcasted_iota(jnp.int32, (32, FMAX), 0) == owners[...]).astype(BF16)
    high, low = split(gain)
    total = jnp.dot(onehot, high, preferred_element_type=F32)
    total = total + jnp.dot(onehot, low, preferred_element_type=F32)
    terms[...] = jnp.broadcast_to(total[:, None, :], (32, 8, CZ))

    @pl.loop(0, count[0] // 8)
    def _(g):
        for r in range(8):
            at = index[g * 8 + r]
            for c in range(COMP):
                ov[c, pl.ds(at, 1), :] = cur[g, pl.ds(c * 8 + r, 1), :]

    copy = pltpu.make_async_copy(ov, out, out_sem)
    copy.start()
    copy.wait()


def heat_kernel(n_gy, terms, out, got, send, recv):
    gx, gy = lax.axis_index("gx"), lax.axis_index("gy")
    barrier = pltpu.get_barrier_semaphore()

    @pl.loop(1, n_gy)
    def _(k):
        pl.semaphore_signal(
            barrier, inc=1, device_id=(gx, lax.rem(gy + k, n_gy)), device_id_type=MESH
        )

    pl.semaphore_wait(barrier, n_gy - 1)

    def copy(k):
        other = lax.rem(gy + k, n_gy)
        return pltpu.make_async_remote_copy(
            src_ref=terms.at[other],
            dst_ref=got.at[k],
            send_sem=send.at[k],
            recv_sem=recv.at[k],
            device_id=(gx, other),
            device_id_type=MESH,
        )

    @pl.loop(1, n_gy)
    def _(k):
        copy(k).start()

    got[0] = terms[gy]

    @pl.loop(1, n_gy)
    def _(k):
        copy(k).wait()

    total = jnp.sum(got[:, 0, :], axis=0, keepdims=True)
    out[...] = jnp.sum(total, axis=1, keepdims=True) * (1.0 / math.sqrt(CZ) / math.sqrt(RMAX))


def per_device(n_gx, n_gy, fields, diffusivity, decay_rates, reaction_matrix, owner_index, flame_flag):
    flags = flame_flag.reshape(CH)
    owners = owner_index.reshape(CH)
    rank = jnp.where(flags > 0, jnp.cumsum(flags) - flags, -1)
    count = jnp.sum(flags).reshape(1)
    slots = jnp.arange(FMAX, dtype=jnp.int32)
    code = owners * CH + jnp.arange(CH, dtype=jnp.int32)
    picked = jnp.sum(jnp.where(rank[None, :] == slots[:, None], code[None, :] + 1, 0), axis=1) - 1
    index = jnp.where(picked >= 0, picked % CH, 0)
    slot_owner = jnp.where(picked >= 0, picked // CH, -1).reshape(1, FMAX)
    exact = lax.Precision.HIGHEST
    inv = 1.0 / (1.0 + H_STEP * decay_rates)
    m1 = H_STEP * reaction_matrix * inv[:, None]
    m2 = jnp.dot(m1, m1, precision=exact)
    m3 = jnp.dot(m2, m1, precision=exact)
    every = jnp.concatenate(
        [m1 * inv[None, :], m2 * inv[None, :], m3, m1[9:10], m2[9:10]], axis=0
    )
    high = lax.reduce_precision(every, 8, 7)
    low = lax.reduce_precision(every - high, 8, 7)
    eye = jnp.eye(8, dtype=F32)
    stacked = jnp.concatenate([high, high, low], axis=1)
    matrix = (stacked[:, None, :, None] * eye[None, :, None, :]).reshape(256, 240).astype(BF16)
    inverse = jnp.broadcast_to(jnp.repeat(inv, 8)[:, None], (80, CZ))
    z = jnp.arange(CZ)
    gap = jnp.abs(z[:, None] - z[None, :])
    tap = jnp.where(gap == 0, -6.0, jnp.where(gap == 1, 1.0, 0.0))
    taps = jnp.concatenate([tap, tap], axis=0).astype(BF16)

    shape = (COMP, CX, CY, CZ)
    dma = pltpu.SemaphoreType.DMA
    u2 = pl.pallas_call(
        functools.partial(halo_kernel, n_gx, n_gy),
        out_shape=jax.ShapeDtypeStruct(shape, F32),
        in_specs=[ANY, VMEM, SMEM],
        out_specs=ANY,
        scratch_shapes=[
            pltpu.VMEM((COMP, CX + 4, CY + 16, CZ), F32),
            pltpu.VMEM((COMP, CX + 2, CY + 16, CZ), F32),
            pltpu.VMEM(shape, F32),
            dma,
            dma((8,)),
            dma((8,)),
            dma((3 * COMP,)),
        ],
        compiler_params=pltpu.CompilerParams(
            collective_id=0, has_side_effects=True, vmem_limit_bytes=LIMIT
        ),
        name="halo_diffuse",
    )(fields, taps, diffusivity)
    merged, terms = pl.pallas_call(
        chem_kernel,
        out_shape=(
            jax.ShapeDtypeStruct((COMP, CH, CZ), F32),
            jax.ShapeDtypeStruct((32, 8, CZ), F32),
        ),
        in_specs=[ANY, VMEM, VMEM, SMEM, SMEM, VMEM],
        out_specs=(ANY, VMEM),
        scratch_shapes=[
            pltpu.VMEM((COMP, CH, CZ), F32),
            pltpu.VMEM((COMP, CH, CZ), F32),
            pltpu.VMEM((FMAX // 8, 80, CZ), F32),
            pltpu.VMEM((FMAX // 8, 8, CZ), F32),
            dma((CH // CHUNK,)),
            dma,
        ],
        compiler_params=pltpu.CompilerParams(vmem_limit_bytes=LIMIT),
        name="chemistry",
    )(u2.reshape(COMP, CH, CZ), matrix, inverse, index, count, slot_owner)
    heat = pl.pallas_call(
        functools.partial(heat_kernel, n_gy),
        out_shape=jax.ShapeDtypeStruct((1, 1), F32),
        in_specs=[VMEM],
        out_specs=VMEM,
        scratch_shapes=[pltpu.VMEM((n_gy, 8, CZ), F32), dma((n_gy,)), dma((n_gy,))],
        compiler_params=pltpu.CompilerParams(
            collective_id=1, has_side_effects=True, vmem_limit_bytes=LIMIT
        ),
        name="owner_sum",
    )(terms)
    return merged.reshape(shape), heat


def solution(mesh):
    return jax.shard_map(
        functools.partial(per_device, mesh.shape["gx"], mesh.shape["gy"]),
        mesh=mesh,
        in_specs=(
            P(None, "gx", "gy", None),
            P(),
            P(),
            P(),
            P("gx", "gy", None),
            P("gx", "gy", None),
        ),
        out_specs=(P(None, "gx", "gy", None), P("gx", "gy")),
        check_vma=False,
    )
```

```python
import functools
import math

import jax
import jax.numpy as jnp
from jax import lax
from jax.experimental import pallas as pl
from jax.experimental.pallas import tpu as pltpu
from jax.sharding import PartitionSpec as P

H_STEP = 0.2
FLAME_SUB = 10
COMP = 10
CX, CY, CZ = 16, 64, 128
CH = CX * CY
FMAX = 256
RMAX = 60
EARLY = 160
LATE = 96
CHUNK = 128
COOL_EACH = 6

F32, BF16 = jnp.float32, jnp.bfloat16
MESH = pl.DeviceIdType.MESH
VMEM = pl.BlockSpec(memory_space=pltpu.VMEM)
SMEM = pl.BlockSpec(memory_space=pltpu.SMEM)
ANY = pl.BlockSpec(memory_space=pl.ANY)
LIMIT = 56 << 20


def split(values):
    high = values.astype(BF16)
    low = (values - high.astype(F32)).astype(BF16)
    return high, low


def tables(reaction, decay, flags, owners, taps, matrix, inverse, lists, late, pad):
    exact = lax.Precision.HIGHEST
    iota = lax.broadcasted_iota
    one = jnp.float32(1.0)
    gap = jnp.abs((iota(jnp.int32, (2 * CZ, CZ), 0) & (CZ - 1)) - iota(jnp.int32, (2 * CZ, CZ), 1))
    taps[...] = jnp.where(gap == 0, -6.0, jnp.where(gap == 1, 1.0, 0.0)).astype(BF16)

    shares = [one / (one + H_STEP * jnp.full((8, CZ), decay[c], F32)) for c in range(COMP)]
    for c in range(COMP):
        inverse[pl.ds(8 * c, 8), :] = shares[c]
    sub, lane = iota(jnp.int32, (16, CZ), 0), iota(jnp.int32, (16, CZ), 1)
    by_row = jnp.zeros((16, CZ), F32)
    by_lane = jnp.zeros((16, CZ), F32)
    for c in range(COMP):
        share = jnp.concatenate([shares[c], shares[c]], axis=0)
        by_row = jnp.where(sub == c, share, by_row)
        by_lane = jnp.where(lane == c, share, by_lane)
    pad[...] = jnp.zeros((CZ, CZ), F32)
    pad[0:COMP, 0:COMP] = reaction[...]
    m1 = H_STEP * pad[0:16, :] * by_row
    pad[0:16, :] = m1
    full = pad[...]
    m2 = jnp.dot(m1, full, precision=exact, preferred_element_type=F32)
    m3 = jnp.dot(m2, full, precision=exact, preferred_element_type=F32)
    d1, d2 = m1 * by_lane, m2 * by_lane
    every = jnp.concatenate([d1, d2, m3, m1, m2], axis=0)
    high, low = split(every)
    row = iota(jnp.int32, (256, 80), 0) >> 3
    source = row + 6 * (row >= 10).astype(jnp.int32) + 6 * (row >= 20).astype(jnp.int32)
    source = jnp.where(row == 30, 48 + 9, jnp.where(row == 31, 64 + 9, source))
    up = (source == iota(jnp.int32, (256, 80), 1)).astype(BF16)
    column = iota(jnp.int32, (CZ, 240), 1)
    third = (column >= 80).astype(jnp.int32) + (column >= 160).astype(jnp.int32)
    across = (((column - 80 * third) >> 3) == iota(jnp.int32, (CZ, 240), 0)).astype(BF16)
    spread = [
        jnp.dot(
            jnp.dot(up, part, preferred_element_type=F32).astype(BF16),
            across,
            preferred_element_type=F32,
        )
        for part in (high, low)
    ]
    r, n = iota(jnp.int32, (256, 240), 0), iota(jnp.int32, (256, 240), 1)
    value = jnp.where(n < 160, spread[0], spread[1])
    matrix[...] = jnp.where((r & 7) == (n & 7), value, 0.0).astype(BF16)

    flame = flags[...].astype(F32)
    upper = (iota(jnp.int32, (CZ, CZ), 0) <= iota(jnp.int32, (CZ, CZ), 1)).astype(BF16)
    count = jnp.dot(flame.astype(BF16), upper, preferred_element_type=F32)
    total = jnp.dot(flame.astype(BF16), jnp.ones((CZ, CZ), BF16), preferred_element_type=F32)
    inner = jnp.zeros((1, CZ), F32)
    keys = [None] * 8
    for k in range(1, 7):
        keys[k] = count[k : k + 1] - 1.0 + inner
        inner = inner + total[k : k + 1]
    rest = jnp.maximum(inner - EARLY, 0.0)
    keys[0] = count[0:1] - 1.0 + rest
    keys[7] = count[7:8] - 1.0 + rest + total[0:1]
    keys = jnp.concatenate(keys, axis=0)
    which = iota(jnp.int32, (8, CZ), 0)
    outer = (which == 0) | (which == 7)
    on = flame > 0.0
    early = jnp.where(on & ~outer & (keys < EARLY), keys, -1.0)
    after = jnp.where(outer, keys, keys - EARLY)
    after = jnp.where(on & (after >= 0.0), after, -1.0)
    slot = iota(jnp.int32, (FMAX, CZ), 0).astype(F32)
    label = iota(jnp.int32, (8, CZ), 0)
    here = iota(jnp.int32, (8, CZ), 1).astype(F32)
    owner = owners[...].astype(F32)

    def listed(key):
        got = jnp.zeros((8, FMAX), F32)
        for k in range(8):
            hit = (slot == key[k : k + 1]).astype(BF16)
            facts = jnp.where(label == 0, here, jnp.where(label == 1, owner[k : k + 1], 1.0))
            facts = jnp.where(label == 3, float(k), facts)
            got = got + lax.dot_general(
                facts.astype(BF16), hit, (((1,), (1,)), ((), ())), preferred_element_type=F32
            )
        valid = got[2:3]
        index = got[3:4] * float(CZ) + got[0:1] + (1.0 - valid) * float(CZ)
        who = got[1:2] + valid - 1.0
        number = jnp.sum(valid, axis=1, keepdims=True) + jnp.zeros((1, FMAX), F32)
        zero = jnp.zeros((1, FMAX), F32)
        rows = [index, who, number, zero, zero, zero, zero, zero]
        return jnp.concatenate(rows, axis=0).astype(jnp.int32)

    lists[...] = listed(early)
    late[...] = listed(after)


def halo_kernel(
    n_gx, n_gy, fields, diff, reaction, decay, flags, owners,
    out, hot, gain, matrix, inverse, lists, late,
    ext, mid, res, taps, pad, where, first_t, in_sem, send, recv, out_sem, list_sem,
):
    gx, gy = lax.axis_index("gx"), lax.axis_index("gy")
    xm, xp = lax.rem(gx + n_gx - 1, n_gx), lax.rem(gx + 1, n_gx)
    ym, yp = lax.rem(gy + n_gy - 1, n_gy), lax.rem(gy + 1, n_gy)
    load = pltpu.make_async_copy(fields, ext.at[:, pl.ds(2, CX), pl.ds(8, CY), :], in_sem)
    load.start()
    targets = [
        (xp, gy), (xm, gy), (gx, yp), (gx, ym), (xp, yp), (xp, ym), (xm, yp), (xm, ym),
    ]
    barrier = pltpu.get_barrier_semaphore()
    for target in targets:
        pl.semaphore_signal(barrier, inc=1, device_id=target, device_id_type=MESH)
    pl.semaphore_wait(barrier, 8)
    ranges = [
        ((CX - 2, 2), (0, CY), (0, 8)),
        ((0, 2), (0, CY), (CX + 2, 8)),
        ((0, CX), (CY - 2, 2), (2, 6)),
        ((0, CX), (0, 2), (2, CY + 8)),
        ((CX - 1, 1), (CY - 1, 1), (1, 7)),
        ((CX - 1, 1), (0, 1), (1, CY + 8)),
        ((0, 1), (CY - 1, 1), (CX + 2, 7)),
        ((0, 1), (0, 1), (CX + 2, CY + 8)),
    ]
    copies = []
    for number, (target, (xs, ys, (dx, dy))) in enumerate(zip(targets, ranges)):
        copies.append(
            pltpu.make_async_remote_copy(
                src_ref=fields.at[:, pl.ds(*xs), pl.ds(*ys), :],
                dst_ref=ext.at[:, pl.ds(dx, xs[1]), pl.ds(dy, ys[1]), :],
                send_sem=send.at[number],
                recv_sem=recv.at[number],
                device_id=target,
                device_id_type=MESH,
            )
        )
    for number in (0, 1, 2, 3, 4, 5, 6, 7):
        copies[number].start()
    tables(reaction, decay, flags, owners, taps, matrix, inverse, lists, late, pad)
    listing = pltpu.make_async_copy(lists, where, list_sem)
    listing.start()
    load.wait()

    def first(c, x, count):
        d = diff[c]
        shape = (count * 80, CZ)
        v = ext[c, pl.ds(x, count)].reshape(shape)
        near = ext[c, pl.ds(x - 1, count)].reshape(shape) + ext[c, pl.ds(x + 1, count)].reshape(shape)
        near = near + pltpu.roll(v, 1, 0) + pltpu.roll(v, shape[0] - 1, 0)
        near = near + jnp.dot(
            jnp.concatenate(split(v), axis=1), taps[...], preferred_element_type=F32
        )
        mid[c, pl.ds(x - 1, count)] = (v + d * near).reshape(count, 80, CZ)

    def second(c, x, count):
        d = diff[c]
        shape = (count * 80, CZ)
        v = mid[c, pl.ds(x + 1, count)].reshape(shape)
        near = mid[c, pl.ds(x, count)].reshape(shape) + mid[c, pl.ds(x + 2, count)].reshape(shape)
        near = near + pltpu.roll(v, 1, 0) + pltpu.roll(v, shape[0] - 1, 0)
        near = near + jnp.dot(
            jnp.concatenate(split(v), axis=1), taps[...], preferred_element_type=F32
        )
        new = (v + d * near).reshape(count, 80, CZ)[:, 8 : 8 + CY]
        res[c, pl.ds(x * CY, count * CY)] = new.reshape(count * CY, CZ)

    def clear(ref, xs, ys):
        @pl.loop(0, COMP)
        def _(c):
            ref[c, pl.ds(*xs), pl.ds(*ys), :] = jnp.zeros((xs[1], ys[1], CZ), F32)

    def edges(ref, xs):
        @pl.when(gy == 0)
        def _():
            clear(ref, xs, (0, 8))

        @pl.when(gy == n_gy - 1)
        def _():
            clear(ref, xs, (CY + 8, 8))

    copies[2].wait_recv()
    copies[3].wait_recv()
    edges(ext, (2, CX))

    @pl.loop(0, COMP)
    def _(c):
        first(c, 3, 7)
        first(c, 10, 7)

    edges(mid, (2, CX - 2))

    @pl.loop(0, COMP)
    def _(c):
        second(c, 2, 6)
        second(c, 8, 6)
        pltpu.make_async_copy(
            res.at[c, pl.ds((2) * CY, (CX - 4) * CY)], out.at[c, pl.ds((2) * CY, (CX - 4) * CY)], out_sem.at[c]
        ).start()

    listing.wait()

    @pl.loop(0, EARLY // 8)
    def _(g):
        for r in range(8):
            at = jnp.clip(where[0, g * 8 + r], 0, CH - 1)
            for c in range(COMP):
                hot[g, pl.ds(c * 8 + r, 1), :] = res[c, pl.ds(at, 1), :]
        first_t[g] = hot[g, 72:80, :]

    inv = inverse[...]
    inv = jnp.concatenate([inv, inv], axis=1)

    @pl.loop(0, FLAME_SUB)
    def _(s):
        for t in range(EARLY // 16):
            flame_tile(hot, t, matrix, inv)

    gain[...] = hot[:, 72:80, :] - first_t[...]

    for number in (0, 1, 4, 5, 6, 7):
        copies[number].wait_recv()
    edges(ext, (1, 1))
    edges(ext, (CX + 2, 1))

    @pl.when(gx == 0)
    def _():
        clear(ext, (0, 2), (0, CY + 16))

    @pl.when(gx == n_gx - 1)
    def _():
        clear(ext, (CX + 2, 2), (0, CY + 16))

    @pl.loop(0, COMP)
    def _(c):
        first(c, 1, 2)
        first(c, CX + 1, 2)

    edges(mid, (1, 1))
    edges(mid, (CX, 1))

    @pl.when(gx == 0)
    def _():
        clear(mid, (0, 1), (0, CY + 16))

    @pl.when(gx == n_gx - 1)
    def _():
        clear(mid, (CX + 1, 1), (0, CY + 16))

    @pl.loop(0, COMP)
    def _(c):
        second(c, 0, 2)
        second(c, CX - 2, 2)
        pltpu.make_async_copy(
            res.at[c, pl.ds((0) * CY, (2) * CY)], out.at[c, pl.ds((0) * CY, (2) * CY)], out_sem.at[COMP + c]
        ).start()
        pltpu.make_async_copy(
            res.at[c, pl.ds((CX - 2) * CY, (2) * CY)], out.at[c, pl.ds((CX - 2) * CY, (2) * CY)], out_sem.at[2 * COMP + c]
        ).start()

    for copy in copies:
        copy.wait_send()

    @pl.loop(0, COMP)
    def _(c):
        pltpu.make_async_copy(
            res.at[c, pl.ds((2) * CY, (CX - 4) * CY)], out.at[c, pl.ds((2) * CY, (CX - 4) * CY)], out_sem.at[c]
        ).wait()
        pltpu.make_async_copy(
            res.at[c, pl.ds((0) * CY, (2) * CY)], out.at[c, pl.ds((0) * CY, (2) * CY)], out_sem.at[COMP + c]
        ).wait()
        pltpu.make_async_copy(
            res.at[c, pl.ds((CX - 2) * CY, (2) * CY)], out.at[c, pl.ds((CX - 2) * CY, (2) * CY)], out_sem.at[2 * COMP + c]
        ).wait()


def sigmoid(x):
    return 0.5 * jnp.tanh(0.5 * x) + 0.5


def substep(state, matrix, inverse):
    high, low = split(state)
    r = jnp.dot(matrix, jnp.concatenate([high, low, high], axis=0), preferred_element_type=F32)
    last = state[72:80]
    base = last * inverse[72:80]
    g0 = sigmoid(last)
    g1 = sigmoid(base + g0 * r[240:248])
    g2 = sigmoid(base + g1 * (r[72:80] + g0 * r[248:256]))
    rows = []
    for c in range(COMP):
        at = 8 * c
        inner = r[80 + at : 88 + at] + g0 * r[160 + at : 168 + at]
        rows.append(state[at : at + 8] * inverse[at : at + 8] + g2 * (r[at : at + 8] + g1 * inner))
    return rows


def flame_tile(cur, t, matrix, inv):
    rows = substep(jnp.concatenate([cur[2 * t], cur[2 * t + 1]], axis=1), matrix[...], inv)
    new = jnp.concatenate(rows, axis=0)
    cur[2 * t] = new[:, :CZ]
    cur[2 * t + 1] = new[:, CZ:]


def chem_kernel(
    u2, hot, gain1, matrix, inverse, index1, index2, lists1, lists2,
    out, terms, uv, ov, cur, gain2, in_sem, out_sem,
):
    def fetch(k):
        part = pl.ds(k * CHUNK, CHUNK)
        return pltpu.make_async_copy(u2.at[:, part, :], uv.at[:, part, :], in_sem.at[k])

    for k in range(CH // CHUNK):
        fetch(k).start()
    inv = inverse[...]
    inv = jnp.concatenate([inv, inv], axis=1)

    def cool_tile(t):
        at = [pl.multiple_of(t * 16 + w * 8, 8) for w in range(2)]
        groups = [
            jnp.concatenate([uv[c, pl.ds(a, 8), :] for c in range(COMP)], axis=0) for a in at
        ]
        rows = substep(jnp.concatenate(groups, axis=1), matrix[...], inv)
        for w in range(2):
            for c in range(COMP):
                ov[c, pl.ds(at[w], 8), :] = rows[c][:, w * CZ : (w + 1) * CZ]

    for k in range(CH // CHUNK):
        fetch(k).wait()
    gain2[...] = jnp.zeros_like(gain2)
    number = jnp.clip(index2[2, 0], 0, FMAX)

    def gather(j):
        @pl.loop(0, LATE // 8)
        def _(g):
            for r in range(8):
                at = index2[0, jnp.minimum(j * LATE + g * 8 + r, FMAX - 1)]
                for c in range(COMP):
                    cur[g, pl.ds(c * 8 + r, 1), :] = uv[c, pl.ds(at, 1), :]
            gain2[j * (LATE // 8) + g] = -cur[g, 72:80, :]

    def scatter(j):
        @pl.loop(0, LATE // 8)
        def _(g):
            gain2[j * (LATE // 8) + g] = gain2[j * (LATE // 8) + g] + cur[g, 72:80, :]

        def one(p, carry):
            at = index2[0, j * LATE + p]
            for c in range(COMP):
                ov[c, pl.ds(at, 1), :] = cur[p >> 3, pl.ds(c * 8 + (p & 7), 1), :]
            return carry

        lax.fori_loop(0, jnp.minimum(number - j * LATE, LATE), one, 0)

    gather(0)

    @pl.loop(0, FLAME_SUB)
    def _(s):
        for t in range(LATE // 16):
            flame_tile(cur, t, matrix, inv)
        for t in range(COOL_EACH):
            cool_tile(s * COOL_EACH + t)

    for t in range(FLAME_SUB * COOL_EACH, CH // 16):
        cool_tile(t)
    scatter(0)

    @pl.loop(1, (number + LATE - 1) // LATE)
    def _(j):
        gather(j)

        @pl.loop(0, FLAME_SUB)
        def _(s):
            for t in range(LATE // 16):
                flame_tile(cur, t, matrix, inv)

        scatter(j)

    def early(p, carry):
        at = index1[0, p]
        for c in range(COMP):
            ov[c, pl.ds(at, 1), :] = hot[p >> 3, pl.ds(c * 8 + (p & 7), 1), :]
        return carry

    lax.fori_loop(0, jnp.clip(index1[2, 0], 0, EARLY), early, 0)
    copy = pltpu.make_async_copy(ov, out, out_sem)
    copy.start()

    row = lax.broadcasted_iota(jnp.int32, (64, FMAX), 0)
    owner = jnp.where((row & 7) < 4, (row & 7) * 8 + (row >> 3), -2)
    total = jnp.zeros((64, CZ), F32)
    for lists, values, count in (
        (lists1, gain1[...].reshape(EARLY, CZ), EARLY),
        (lists2, gain2[0 : FMAX // 8].reshape(FMAX, CZ), FMAX),
    ):
        onehot = (owner[:, :count] == lists[1:2, :count]).astype(BF16)
        for part in split(values):
            total = total + jnp.dot(onehot, part, preferred_element_type=F32)
    terms[...] = total.reshape(8, 8, CZ)
    copy.wait()


def heat_kernel(n_gy, terms, out, got, part, back, send, recv):
    gx, gy = lax.axis_index("gx"), lax.axis_index("gy")
    high = n_gy // 8
    plane = gy // 8
    place = gy - 8 * plane
    near = []
    for k in range(1, 8):
        other = place + k
        near.append(jnp.where(other >= 8, other - 8, other))
    far = []
    for k in range(1, high):
        other = plane + k
        far.append(jnp.where(other >= high, other - high, other))
    barrier = pltpu.get_barrier_semaphore()
    for other in near:
        pl.semaphore_signal(
            barrier, inc=1, device_id=(gx, plane * 8 + other), device_id_type=MESH
        )
    for other in far:
        pl.semaphore_signal(
            barrier, inc=1, device_id=(gx, other * 8 + place), device_id_type=MESH
        )
    pl.semaphore_wait(barrier, 7 + high - 1)

    copies = []
    for k, other in enumerate(near):
        copy = pltpu.make_async_remote_copy(
            src_ref=terms.at[other],
            dst_ref=got.at[k],
            send_sem=send.at[k],
            recv_sem=recv.at[k],
            device_id=(gx, plane * 8 + other),
            device_id_type=MESH,
        )
        copy.start()
        copies.append(copy)
    total = terms[place]
    for k, copy in enumerate(copies):
        copy.wait_recv()
        total = total + got[k]
    part[...] = total
    row = lax.broadcasted_iota(jnp.int32, (8, CZ), 0)
    again = []
    for k, other in enumerate(far):
        copy = pltpu.make_async_remote_copy(
            src_ref=part,
            dst_ref=back.at[k],
            send_sem=send.at[7 + k],
            recv_sem=recv.at[7 + k],
            device_id=(gx, other * 8 + place),
            device_id_type=MESH,
        )
        copy.start()
        again.append(copy)
    for k, copy in enumerate(again):
        copy.wait_recv()
        total = total + back[k]
    total = jnp.where(row == plane, total, 0.0)
    total = jnp.sum(jnp.sum(total, axis=0, keepdims=True), axis=1, keepdims=True)
    out[...] = total * (1.0 / math.sqrt(CZ) / math.sqrt(RMAX))
    for copy in copies + again:
        copy.wait_send()


def per_device(n_gx, n_gy, fields, diffusivity, decay_rates, reaction_matrix, owner_index, flame_flag):
    shape = (COMP, CH, CZ)
    dma = pltpu.SemaphoreType.DMA
    as_f32 = lambda *dims: jax.ShapeDtypeStruct(dims, F32)
    as_i32 = lambda *dims: jax.ShapeDtypeStruct(dims, jnp.int32)
    u2, hot, gain, matrix, inverse, lists, late = pl.pallas_call(
        functools.partial(halo_kernel, n_gx, n_gy),
        out_shape=(
            as_f32(*shape),
            as_f32(EARLY // 8, 80, CZ),
            as_f32(EARLY // 8, 8, CZ),
            jax.ShapeDtypeStruct((256, 240), BF16),
            as_f32(80, CZ),
            as_i32(8, FMAX),
            as_i32(8, FMAX),
        ),
        in_specs=[ANY, SMEM, VMEM, SMEM, VMEM, VMEM],
        out_specs=(ANY,) + (VMEM,) * 6,
        scratch_shapes=[
            pltpu.VMEM((COMP, CX + 4, CY + 16, CZ), F32),
            pltpu.VMEM((COMP, CX + 2, CY + 16, CZ), F32),
            pltpu.VMEM(shape, F32),
            pltpu.VMEM((2 * CZ, CZ), BF16),
            pltpu.VMEM((CZ, CZ), F32),
            pltpu.SMEM((8, FMAX), jnp.int32),
            pltpu.VMEM((EARLY // 8, 8, CZ), F32),
            dma,
            dma((8,)),
            dma((8,)),
            dma((3 * COMP,)),
            dma,
        ],
        compiler_params=pltpu.CompilerParams(
            collective_id=0, has_side_effects=True, vmem_limit_bytes=LIMIT
        ),
        name="halo_diffuse",
    )(
        fields, diffusivity, reaction_matrix, decay_rates,
        flame_flag.reshape(8, CZ), owner_index.reshape(8, CZ),
    )
    chunks = -(-FMAX // LATE)
    merged, terms = pl.pallas_call(
        chem_kernel,
        out_shape=(as_f32(*shape), as_f32(8, 8, CZ)),
        in_specs=[ANY, VMEM, VMEM, VMEM, VMEM, SMEM, SMEM, VMEM, VMEM],
        out_specs=(ANY, VMEM),
        scratch_shapes=[
            pltpu.VMEM(shape, F32),
            pltpu.VMEM(shape, F32),
            pltpu.VMEM((LATE // 8, 80, CZ), F32),
            pltpu.VMEM((chunks * (LATE // 8), 8, CZ), F32),
            dma((CH // CHUNK,)),
            dma,
        ],
        compiler_params=pltpu.CompilerParams(vmem_limit_bytes=LIMIT),
        name="chemistry",
    )(u2, hot, gain, matrix, inverse, lists, late, lists, late)
    heat = pl.pallas_call(
        functools.partial(heat_kernel, n_gy),
        out_shape=as_f32(1, 1),
        in_specs=[VMEM],
        out_specs=VMEM,
        scratch_shapes=[
            pltpu.VMEM((7, 8, CZ), F32),
            pltpu.VMEM((8, CZ), F32),
            pltpu.VMEM((n_gy // 8 - 1, 8, CZ), F32),
            dma((7 + n_gy // 8 - 1,)),
            dma((7 + n_gy // 8 - 1,)),
        ],
        compiler_params=pltpu.CompilerParams(
            collective_id=1, has_side_effects=True, vmem_limit_bytes=LIMIT
        ),
        name="owner_sum",
    )(terms)
    return merged.reshape(COMP, CX, CY, CZ), heat


def solution(mesh):
    return jax.shard_map(
        functools.partial(per_device, mesh.shape["gx"], mesh.shape["gy"]),
        mesh=mesh,
        in_specs=(
            P(None, "gx", "gy", None),
            P(),
            P(),
            P(),
            P("gx", "gy", None),
            P("gx", "gy", None),
        ),
        out_specs=(P(None, "gx", "gy", None), P("gx", "gy")),
        check_vma=False,
    )
```

```python
import functools
import math

import jax
import jax.numpy as jnp
from jax import lax
from jax.experimental import pallas as pl
from jax.experimental.pallas import tpu as pltpu
from jax.sharding import PartitionSpec as P

H_STEP = 0.2
FLAME_SUB = 10
COMP = 10
CX, CY, CZ = 16, 64, 128
CH = CX * CY
FMAX = 256
RMAX = 60
GROUP = 2

F32, BF16 = jnp.float32, jnp.bfloat16
MESH = pl.DeviceIdType.MESH
VMEM = pl.BlockSpec(memory_space=pltpu.VMEM)
SMEM = pl.BlockSpec(memory_space=pltpu.SMEM)
ANY = pl.BlockSpec(memory_space=pl.ANY)
LIMIT = 56 << 20


def split(values):
    high = values.astype(BF16)
    low = (values - high.astype(F32)).astype(BF16)
    return high, low


def tables(reaction, decay, flags, owners, taps, matrix, inverse, lists, pad):
    exact = lax.Precision.HIGHEST
    iota = lax.broadcasted_iota
    one = jnp.float32(1.0)
    gap = jnp.abs((iota(jnp.int32, (2 * CZ, CZ), 0) & (CZ - 1)) - iota(jnp.int32, (2 * CZ, CZ), 1))
    taps[...] = jnp.where(gap == 0, -6.0, jnp.where(gap == 1, 1.0, 0.0)).astype(BF16)

    shares = [one / (one + H_STEP * jnp.full((8, CZ), decay[c], F32)) for c in range(COMP)]
    for c in range(COMP):
        inverse[pl.ds(8 * c, 8), :] = shares[c]
    sub, lane = iota(jnp.int32, (16, CZ), 0), iota(jnp.int32, (16, CZ), 1)
    by_row = jnp.zeros((16, CZ), F32)
    by_lane = jnp.zeros((16, CZ), F32)
    for c in range(COMP):
        share = jnp.concatenate([shares[c], shares[c]], axis=0)
        by_row = jnp.where(sub == c, share, by_row)
        by_lane = jnp.where(lane == c, share, by_lane)
    pad[...] = jnp.zeros((CZ, CZ), F32)
    pad[0:COMP, 0:COMP] = reaction[...]
    m1 = H_STEP * pad[0:16, :] * by_row
    pad[0:16, :] = m1
    full = pad[...]
    m2 = jnp.dot(m1, full, precision=exact, preferred_element_type=F32)
    m3 = jnp.dot(m2, full, precision=exact, preferred_element_type=F32)
    d1, d2 = m1 * by_lane, m2 * by_lane
    every = jnp.concatenate([d1, d2, m3, m1, m2], axis=0)
    high, low = split(every)
    row = iota(jnp.int32, (256, 80), 0) >> 3
    source = row + 6 * (row >= 10).astype(jnp.int32) + 6 * (row >= 20).astype(jnp.int32)
    source = jnp.where(row == 30, 48 + 9, jnp.where(row == 31, 64 + 9, source))
    up = (source == iota(jnp.int32, (256, 80), 1)).astype(BF16)
    column = iota(jnp.int32, (CZ, 240), 1)
    third = (column >= 80).astype(jnp.int32) + (column >= 160).astype(jnp.int32)
    across = (((column - 80 * third) >> 3) == iota(jnp.int32, (CZ, 240), 0)).astype(BF16)
    spread = [
        jnp.dot(
            jnp.dot(up, part, preferred_element_type=F32).astype(BF16),
            across,
            preferred_element_type=F32,
        )
        for part in (high, low)
    ]
    r, n = iota(jnp.int32, (256, 240), 0), iota(jnp.int32, (256, 240), 1)
    value = jnp.where(n < 160, spread[0], spread[1])
    matrix[...] = jnp.where((r & 7) == (n & 7), value, 0.0).astype(BF16)

    flame = flags[...].astype(F32)
    upper = (iota(jnp.int32, (CZ, CZ), 0) <= iota(jnp.int32, (CZ, CZ), 1)).astype(BF16)
    count = jnp.dot(flame.astype(BF16), upper, preferred_element_type=F32)
    total = jnp.dot(flame.astype(BF16), jnp.ones((CZ, CZ), BF16), preferred_element_type=F32)
    before = jnp.zeros((1, CZ), F32)
    keys = []
    for k in range(8):
        keys.append(count[k : k + 1] - 1.0 + before)
        before = before + total[k : k + 1]
    key = jnp.where(flame > 0.0, jnp.concatenate(keys, axis=0), -1.0)
    slot = iota(jnp.int32, (FMAX, CZ), 0).astype(F32)
    label = iota(jnp.int32, (8, CZ), 0)
    here = iota(jnp.int32, (8, CZ), 1).astype(F32)
    owner = owners[...].astype(F32)

    got = jnp.zeros((8, FMAX), F32)
    for k in range(8):
        hit = (slot == key[k : k + 1]).astype(BF16)
        facts = jnp.where(label == 0, here, jnp.where(label == 1, owner[k : k + 1], 1.0))
        facts = jnp.where(label == 3, float(k), facts)
        got = got + lax.dot_general(
            facts.astype(BF16), hit, (((1,), (1,)), ((), ())), preferred_element_type=F32
        )
    valid = got[2:3]
    index = got[3:4] * float(CZ) + got[0:1]
    who = got[1:2] + valid - 1.0
    zero = jnp.zeros((1, FMAX), F32)
    number = jnp.sum(valid, axis=1, keepdims=True) + zero
    below = [
        jnp.sum(jnp.where(index < at, valid, 0.0), axis=1, keepdims=True) + zero
        for at in (CH // 4, CH // 2, 3 * CH // 4)
    ]
    rows = [index, who, number] + below + [zero, zero]
    lists[...] = jnp.concatenate(rows, axis=0).astype(jnp.int32)


def halo_kernel(
    n_gx, n_gy, fields, diff, reaction, decay, flags, owners,
    cool, hot_out, heat, lists,
    hot, ext, mid, res, ov, taps, matrix, inverse, pad, where, first_t, terms, got, part, back,
    in_sem, send, recv, out_sem, list_sem, hot_sem, heat_send, heat_recv,
):
    gx, gy = lax.axis_index("gx"), lax.axis_index("gy")
    xm, xp = lax.rem(gx + n_gx - 1, n_gx), lax.rem(gx + 1, n_gx)
    ym, yp = lax.rem(gy + n_gy - 1, n_gy), lax.rem(gy + 1, n_gy)
    load = pltpu.make_async_copy(fields, ext.at[:, pl.ds(2, CX), pl.ds(8, CY), :], in_sem)
    load.start()
    targets = [
        (xp, gy), (xm, gy), (gx, yp), (gx, ym), (xp, yp), (xp, ym), (xm, yp), (xm, ym),
    ]
    barrier = pltpu.get_barrier_semaphore()
    for target in targets:
        pl.semaphore_signal(barrier, inc=1, device_id=target, device_id_type=MESH)
    planes = n_gy // 8
    plane = gy // 8
    place = gy - 8 * plane
    near_ones, far_ones = [], []
    for k in range(1, 8):
        other = place + k
        near_ones.append(jnp.where(other >= 8, other - 8, other))
    for k in range(1, planes):
        other = plane + k
        far_ones.append(jnp.where(other >= planes, other - planes, other))
    near_ids = [(gx, plane * 8 + other) for other in near_ones]
    far_ids = [(gx, other * 8 + place) for other in far_ones]
    for target in near_ids + far_ids:
        pl.semaphore_signal(barrier, inc=1, device_id=target, device_id_type=MESH)
    pl.semaphore_wait(barrier, 8 + 7 + planes - 1)
    jobs = []
    for first_c in range(0, COMP, GROUP):
        comps = (first_c, GROUP)
        jobs.append((xp, gy, comps, (CX - 2, 2), (0, CY), (0, 8)))
        jobs.append((xm, gy, comps, (0, 2), (0, CY), (CX + 2, 8)))
    faces = len(jobs)
    every = (0, COMP)
    jobs.append((gx, yp, every, (0, CX), (CY - 2, 2), (2, 6)))
    jobs.append((gx, ym, every, (0, CX), (0, 2), (2, CY + 8)))
    jobs.append((xp, yp, every, (CX - 1, 1), (CY - 1, 1), (1, 7)))
    jobs.append((xp, ym, every, (CX - 1, 1), (0, 1), (1, CY + 8)))
    jobs.append((xm, yp, every, (0, 1), (CY - 1, 1), (CX + 2, 7)))
    jobs.append((xm, ym, every, (0, 1), (0, 1), (CX + 2, CY + 8)))
    copies = []
    for number, (to_x, to_y, comps, xs, ys, (dx, dy)) in enumerate(jobs):
        copies.append(
            pltpu.make_async_remote_copy(
                src_ref=fields.at[pl.ds(*comps), pl.ds(*xs), pl.ds(*ys), :],
                dst_ref=ext.at[pl.ds(*comps), pl.ds(dx, xs[1]), pl.ds(dy, ys[1]), :],
                send_sem=send.at[number],
                recv_sem=recv.at[number],
                device_id=(to_x, to_y),
                device_id_type=MESH,
            )
        )
    for number in list(range(faces, faces + 2)) + list(range(faces)) + list(range(faces + 2, faces + 6)):
        copies[number].start()
    tables(reaction, decay, flags, owners, taps, matrix, inverse, lists, pad)
    listing = pltpu.make_async_copy(lists, where, list_sem)
    listing.start()
    load.wait()

    low_x, high_x = gx == 0, gx == n_gx - 1
    low_y, high_y = gy == 0, gy == n_gy - 1

    def lap(v, near):
        rows = v.shape[0]
        near = near + pltpu.roll(v, 1, 0) + pltpu.roll(v, rows - 1, 0)
        return near + jnp.dot(
            jnp.concatenate(split(v), axis=1), taps[...], preferred_element_type=F32
        )

    def masked(planes):
        top = jnp.where(low_y, 0.0, planes[:, 0:8])
        bottom = jnp.where(high_y, 0.0, planes[:, 8 + CY :])
        return jnp.concatenate([top, planes[:, 8 : 8 + CY], bottom], axis=1)

    def first(c, x, count):
        d = diff[c]
        shape = (count * CY, CZ)

        def rows(at):
            return ext[c, pl.ds(at, count), 8 : 8 + CY].reshape(shape)

        v = rows(x)
        new = v + d * lap(v, rows(x - 1) + rows(x + 1))
        mid[c, pl.ds(x - 1, count), 8 : 8 + CY] = new.reshape(count, CY, CZ)

    def rim(c, x, count):
        d = diff[c]

        def rows(at):
            both = [ext[c, pl.ds(at, count), 0:16], ext[c, pl.ds(at, count), CY : CY + 16]]
            return jnp.concatenate(both, axis=1).reshape(count * 32, CZ)

        v = rows(x)
        new = (v + d * lap(v, rows(x - 1) + rows(x + 1))).reshape(count, 32, CZ)
        to = pl.ds(x - 1, count)
        mid[c, to, 0:8] = jnp.where(low_y, 0.0, new[:, 0:8])
        mid[c, to, 8:9] = new[:, 8:9]
        mid[c, to, CY + 7 : CY + 8] = new[:, 23:24]
        mid[c, to, CY + 8 :] = jnp.where(high_y, 0.0, new[:, 24:32])

    def second(c, x, count):
        d = diff[c]
        shape = (count * 80, CZ)
        v = mid[c, pl.ds(x + 1, count)].reshape(shape)
        near = mid[c, pl.ds(x, count)].reshape(shape) + mid[c, pl.ds(x + 2, count)].reshape(shape)
        new = (v + d * lap(v, near)).reshape(count, 80, CZ)[:, 8 : 8 + CY]
        res[c, pl.ds(x * CY, count * CY)] = new.reshape(count * CY, CZ)

    def outer(cs):
        zero = jnp.zeros((80, CZ), F32)
        centre, near = [], []
        for c in cs:
            a, b, e, f = [ext[c, k] for k in range(4)]
            b = jnp.where(low_x, zero, b)
            centre += [b, e]
            near += [a + e, b + f]
            f, e, b, a = [ext[c, CX + k] for k in range(4)]
            b = jnp.where(high_x, zero, b)
            centre += [e, b]
            near += [f + b, e + a]
        centre = jnp.concatenate(centre, axis=0)
        total = lap(centre, jnp.concatenate(near, axis=0))
        centre2, near2 = [], []
        for k, c in enumerate(cs):
            part = slice(k * 320, k * 320 + 320)
            p = masked((centre[part] + diff[c] * total[part]).reshape(4, 80, CZ))
            m0 = jnp.where(low_x, zero, p[0])
            centre2 += [p[1], mid[c, 2]]
            near2 += [m0 + mid[c, 2], p[1] + mid[c, 3]]
            m1 = jnp.where(high_x, zero, p[3])
            centre2 += [mid[c, CX - 1], p[2]]
            near2 += [mid[c, CX - 2] + p[2], mid[c, CX - 1] + m1]
        centre2 = jnp.concatenate(centre2, axis=0)
        total2 = lap(centre2, jnp.concatenate(near2, axis=0))
        for k, c in enumerate(cs):
            part = slice(k * 320, k * 320 + 320)
            new = (centre2[part] + diff[c] * total2[part]).reshape(4, 80, CZ)[:, 8 : 8 + CY]
            res[c, 0 : 2 * CY] = new[0:2].reshape(2 * CY, CZ)
            res[c, (CX - 2) * CY :] = new[2:4].reshape(2 * CY, CZ)

    def clear(ref, xs, ys):
        @pl.loop(0, COMP)
        def _(c):
            ref[c, pl.ds(*xs), pl.ds(*ys), :] = jnp.zeros((xs[1], ys[1], CZ), F32)

    def edges(ref, xs):
        @pl.when(gy == 0)
        def _():
            clear(ref, xs, (0, 8))

        @pl.when(gy == n_gy - 1)
        def _():
            clear(ref, xs, (CY + 8, 8))

    @pl.loop(0, COMP)
    def _(c):
        first(c, 3, 7)
        first(c, 10, 7)

    copies[faces].wait_recv()
    copies[faces + 1].wait_recv()
    edges(ext, (2, CX))

    @pl.loop(0, COMP)
    def _(c):
        rim(c, 3, 14)

    @pl.loop(0, COMP)
    def _(c):
        second(c, 2, 6)
        second(c, 8, 6)

    inv = inverse[...]
    inv = jnp.concatenate([inv, inv], axis=1)

    def cool_tile(t):
        at = [t * 16 + w * 8 for w in range(2)]
        if not isinstance(t, int):
            at = [pl.multiple_of(a, 8) for a in at]
        groups = [
            jnp.concatenate([res[c, pl.ds(a, 8), :] for c in range(COMP)], axis=0) for a in at
        ]
        rows = substep(jnp.concatenate(groups, axis=1), matrix[...], inv)
        for w in range(2):
            for c in range(COMP):
                ov[c, pl.ds(at[w], 8), :] = rows[c][:, w * CZ : (w + 1) * CZ]

    edge = 2 * CY // 16
    inner = CH // 16 - 2 * edge

    @pl.loop(0, inner // 12)
    def _(k):
        for t in range(12):
            cool_tile(edge + k * 12 + t)

    def store(k, start, size):
        where_to = pl.ds(start, size)
        return pltpu.make_async_copy(ov.at[:, where_to, :], cool.at[:, where_to, :], out_sem.at[k])

    stores = [
        store(0, 2 * CY, (CX - 4) * CY), store(1, 0, 2 * CY), store(2, (CX - 2) * CY, 2 * CY),
    ]
    stores[0].start()

    for number in range(faces + 2, faces + 6):
        copies[number].wait_recv()
    edges(ext, (1, 1))
    edges(ext, (CX + 2, 1))

    for group in range(faces // 2):
        copies[2 * group].wait_recv()
        copies[2 * group + 1].wait_recv()
        cs = list(range(group * GROUP, (group + 1) * GROUP))
        outer(cs)

    listing.wait()

    @pl.loop(0, FMAX // 8)
    def _(g):
        for r in range(8):
            at = jnp.clip(where[0, g * 8 + r], 0, CH - 1)
            for c in range(COMP):
                hot[g, pl.ds(c * 8 + r, 1), :] = res[c, pl.ds(at, 1), :]
        first_t[g] = hot[g, 72:80, :]

    @pl.loop(0, FLAME_SUB)
    def _(s):
        for t in range(FMAX // 16):
            flame_tile(hot, t, matrix, inv)

    leaving = pltpu.make_async_copy(hot, hot_out, hot_sem)
    leaving.start()
    gain = (hot[:, 72:80, :] - first_t[...]).reshape(FMAX, CZ)
    row = lax.broadcasted_iota(jnp.int32, (64, FMAX), 0)
    owner = jnp.where((row & 7) < planes, (row & 7) * 8 + (row >> 3), -2)
    onehot = (owner == lists[1:2, :]).astype(BF16)
    total = jnp.zeros((64, CZ), F32)
    for piece in split(gain):
        total = total + jnp.dot(onehot, piece, preferred_element_type=F32)
    terms[...] = total.reshape(8, 8, CZ)

    sums = []
    for k, (other, target) in enumerate(zip(near_ones, near_ids)):
        copy = pltpu.make_async_remote_copy(
            src_ref=terms.at[other],
            dst_ref=got.at[k],
            send_sem=heat_send.at[k],
            recv_sem=heat_recv.at[k],
            device_id=target,
            device_id_type=MESH,
        )
        copy.start()
        sums.append(copy)
    for t in range(edge):
        cool_tile(t)
    stores[1].start()
    total = terms[place]
    for k in range(7):
        sums[k].wait_recv()
        total = total + got[k]
    part[...] = total
    for k, target in enumerate(far_ids):
        copy = pltpu.make_async_remote_copy(
            src_ref=part,
            dst_ref=back.at[k],
            send_sem=heat_send.at[7 + k],
            recv_sem=heat_recv.at[7 + k],
            device_id=target,
            device_id_type=MESH,
        )
        copy.start()
        sums.append(copy)
    for t in range(edge):
        cool_tile(edge + inner + t)
    stores[2].start()
    for k in range(planes - 1):
        sums[7 + k].wait_recv()
        total = total + back[k]
    total = jnp.where(lax.broadcasted_iota(jnp.int32, (8, CZ), 0) == plane, total, 0.0)
    total = jnp.sum(jnp.sum(total, axis=0, keepdims=True), axis=1, keepdims=True)
    heat[...] = total * (1.0 / math.sqrt(CZ) / math.sqrt(RMAX))
    for copy in copies + sums:
        copy.wait_send()
    leaving.wait()
    for copy in stores:
        copy.wait()


def sigmoid(x):
    return 0.5 * jnp.tanh(0.5 * x) + 0.5


def substep(state, matrix, inverse):
    high, low = split(state)
    r = jnp.dot(matrix, jnp.concatenate([high, low, high], axis=0), preferred_element_type=F32)
    last = state[72:80]
    base = last * inverse[72:80]
    g0 = sigmoid(last)
    g1 = sigmoid(base + g0 * r[240:248])
    g2 = sigmoid(base + g1 * (r[72:80] + g0 * r[248:256]))
    rows = []
    for c in range(COMP):
        at = 8 * c
        inner = r[80 + at : 88 + at] + g0 * r[160 + at : 168 + at]
        rows.append(state[at : at + 8] * inverse[at : at + 8] + g2 * (r[at : at + 8] + g1 * inner))
    return rows


def flame_tile(cur, t, matrix, inv):
    rows = substep(jnp.concatenate([cur[2 * t], cur[2 * t + 1]], axis=1), matrix[...], inv)
    new = jnp.concatenate(rows, axis=0)
    cur[2 * t] = new[:, :CZ]
    cur[2 * t + 1] = new[:, CZ:]


def merge_kernel(cool, hot_in, index, out, ov, hot, in_sem, hot_sem, out_sem):
    quarter = CH // 4

    def fetch(k):
        at = pl.ds(k * quarter, quarter)
        return pltpu.make_async_copy(cool.at[:, at, :], ov.at[:, at, :], in_sem.at[k])

    def flush(k):
        at = pl.ds(k * quarter, quarter)
        return pltpu.make_async_copy(ov.at[:, at, :], out.at[:, at, :], out_sem.at[k])

    flames = pltpu.make_async_copy(hot_in, hot, hot_sem)
    fetch(0).start()
    flames.start()
    for k in range(1, 4):
        fetch(k).start()
    flames.wait()
    start = 0
    for k in range(4):
        stop = jnp.clip(index[3 + k, 0] if k < 3 else index[2, 0], 0, FMAX)
        fetch(k).wait()

        @pl.loop(0, (jnp.maximum(stop - start, 0) + 7) // 8)
        def _(g, start=start, stop=stop):
            for r in range(8):
                p = jnp.minimum(start + g * 8 + r, stop - 1)
                at = index[0, p]
                for c in range(COMP):
                    ov[c, pl.ds(at, 1), :] = hot[p >> 3, pl.ds(c * 8 + (p & 7), 1), :]

        start = stop
        flush(k).start()
    for k in range(4):
        flush(k).wait()


def per_device(n_gx, n_gy, fields, diffusivity, decay_rates, reaction_matrix, owner_index, flame_flag):
    shape = (COMP, CH, CZ)
    groups = FMAX // 8
    faces = 2 * (COMP // GROUP)
    partners = 7 + n_gy // 8 - 1
    dma = pltpu.SemaphoreType.DMA
    as_f32 = lambda *dims: jax.ShapeDtypeStruct(dims, F32)
    cool, hot, heat, lists = pl.pallas_call(
        functools.partial(halo_kernel, n_gx, n_gy),
        out_shape=(
            as_f32(*shape),
            as_f32(groups, 80, CZ),
            as_f32(1, 1),
            jax.ShapeDtypeStruct((8, FMAX), jnp.int32),
        ),
        in_specs=[ANY, SMEM, VMEM, SMEM, VMEM, VMEM],
        out_specs=(ANY, ANY, VMEM, VMEM),
        scratch_shapes=[
            pltpu.VMEM((groups, 80, CZ), F32),
            pltpu.VMEM((COMP, CX + 4, CY + 16, CZ), F32),
            pltpu.VMEM((COMP, CX + 2, CY + 16, CZ), F32),
            pltpu.VMEM(shape, F32),
            pltpu.VMEM(shape, F32),
            pltpu.VMEM((2 * CZ, CZ), BF16),
            pltpu.VMEM((256, 240), BF16),
            pltpu.VMEM((80, CZ), F32),
            pltpu.VMEM((CZ, CZ), F32),
            pltpu.SMEM((8, FMAX), jnp.int32),
            pltpu.VMEM((groups, 8, CZ), F32),
            pltpu.VMEM((8, 8, CZ), F32),
            pltpu.VMEM((7, 8, CZ), F32),
            pltpu.VMEM((8, CZ), F32),
            pltpu.VMEM((n_gy // 8 - 1, 8, CZ), F32),
            dma,
            dma((faces + 6,)),
            dma((faces + 6,)),
            dma((3,)),
            dma,
            dma,
            dma((partners,)),
            dma((partners,)),
        ],
        compiler_params=pltpu.CompilerParams(
            collective_id=0, has_side_effects=True, vmem_limit_bytes=LIMIT
        ),
        name="halo_diffuse_react",
    )(
        fields, diffusivity, reaction_matrix, decay_rates,
        flame_flag.reshape(8, CZ), owner_index.reshape(8, CZ),
    )
    merged = pl.pallas_call(
        merge_kernel,
        out_shape=as_f32(*shape),
        in_specs=[ANY, ANY, SMEM],
        out_specs=ANY,
        scratch_shapes=[
            pltpu.VMEM(shape, F32),
            pltpu.VMEM((groups, 80, CZ), F32),
            dma((4,)),
            dma,
            dma((4,)),
        ],
        compiler_params=pltpu.CompilerParams(vmem_limit_bytes=LIMIT),
        name="merge_flames",
    )(cool, hot, lists)
    return merged.reshape(COMP, CX, CY, CZ), heat


def solution(mesh):
    return jax.shard_map(
        functools.partial(per_device, mesh.shape["gx"], mesh.shape["gy"]),
        mesh=mesh,
        in_specs=(
            P(None, "gx", "gy", None),
            P(),
            P(),
            P(),
            P("gx", "gy", None),
            P("gx", "gy", None),
        ),
        out_specs=(P(None, "gx", "gy", None), P("gx", "gy")),
        check_vma=False,
    )
```

```python
import functools
import math

import jax
import jax.numpy as jnp
from jax import lax
from jax.experimental import pallas as pl
from jax.experimental.pallas import tpu as pltpu
from jax.sharding import PartitionSpec as P

H_STEP = 0.2
FLAME_SUB = 10
COMP = 10
CX, CY, CZ = 16, 64, 128
CH = CX * CY
FMAX = 256
RMAX = 60
GROUP = 5

F32, BF16 = jnp.float32, jnp.bfloat16
MESH = pl.DeviceIdType.MESH
VMEM = pl.BlockSpec(memory_space=pltpu.VMEM)
SMEM = pl.BlockSpec(memory_space=pltpu.SMEM)
ANY = pl.BlockSpec(memory_space=pl.ANY)
LIMIT = 56 << 20


def split(values):
    high = values.astype(BF16)
    low = (values - high.astype(F32)).astype(BF16)
    return high, low


def tables(reaction, decay, flags, owners, taps, matrix, inverse, lists, pad):
    exact = lax.Precision.HIGHEST
    iota = lax.broadcasted_iota
    one = jnp.float32(1.0)
    gap = jnp.abs((iota(jnp.int32, (2 * CZ, CZ), 0) & (CZ - 1)) - iota(jnp.int32, (2 * CZ, CZ), 1))
    taps[...] = jnp.where(gap == 0, -6.0, jnp.where(gap == 1, 1.0, 0.0)).astype(BF16)

    shares = [one / (one + H_STEP * jnp.full((8, CZ), decay[c], F32)) for c in range(COMP)]
    for c in range(COMP):
        inverse[pl.ds(8 * c, 8), :] = shares[c]
    sub, lane = iota(jnp.int32, (16, CZ), 0), iota(jnp.int32, (16, CZ), 1)
    by_row = jnp.zeros((16, CZ), F32)
    by_lane = jnp.zeros((16, CZ), F32)
    for c in range(COMP):
        share = jnp.concatenate([shares[c], shares[c]], axis=0)
        by_row = jnp.where(sub == c, share, by_row)
        by_lane = jnp.where(lane == c, share, by_lane)
    pad[...] = jnp.zeros((CZ, CZ), F32)
    pad[0:COMP, 0:COMP] = reaction[...]
    m1 = H_STEP * pad[0:16, :] * by_row
    pad[0:16, :] = m1
    full = pad[...]
    m2 = jnp.dot(m1, full, precision=exact, preferred_element_type=F32)
    m3 = jnp.dot(m2, full, precision=exact, preferred_element_type=F32)
    d1, d2 = m1 * by_lane, m2 * by_lane
    every = jnp.concatenate([d1, d2, m3, m1, m2], axis=0)
    high, low = split(every)
    row = iota(jnp.int32, (256, 80), 0) >> 3
    source = row + 6 * (row >= 10).astype(jnp.int32) + 6 * (row >= 20).astype(jnp.int32)
    source = jnp.where(row == 30, 48 + 9, jnp.where(row == 31, 64 + 9, source))
    up = (source == iota(jnp.int32, (256, 80), 1)).astype(BF16)
    column = iota(jnp.int32, (CZ, 240), 1)
    third = (column >= 80).astype(jnp.int32) + (column >= 160).astype(jnp.int32)
    across = (((column - 80 * third) >> 3) == iota(jnp.int32, (CZ, 240), 0)).astype(BF16)
    spread = [
        jnp.dot(
            jnp.dot(up, part, preferred_element_type=F32).astype(BF16),
            across,
            preferred_element_type=F32,
        )
        for part in (high, low)
    ]
    r, n = iota(jnp.int32, (256, 240), 0), iota(jnp.int32, (256, 240), 1)
    value = jnp.where(n < 160, spread[0], spread[1])
    matrix[...] = jnp.where((r & 7) == (n & 7), value, 0.0).astype(BF16)

    flame = flags[...].astype(F32)
    upper = (iota(jnp.int32, (CZ, CZ), 0) <= iota(jnp.int32, (CZ, CZ), 1)).astype(BF16)
    count = jnp.dot(flame.astype(BF16), upper, preferred_element_type=F32)
    total = jnp.dot(flame.astype(BF16), jnp.ones((CZ, CZ), BF16), preferred_element_type=F32)
    before = jnp.zeros((1, CZ), F32)
    keys = []
    for k in range(8):
        keys.append(count[k : k + 1] - 1.0 + before)
        before = before + total[k : k + 1]
    key = jnp.where(flame > 0.0, jnp.concatenate(keys, axis=0), -1.0)
    slot = iota(jnp.int32, (FMAX, CZ), 0).astype(F32)
    label = iota(jnp.int32, (8, CZ), 0)
    here = iota(jnp.int32, (8, CZ), 1).astype(F32)
    owner = owners[...].astype(F32)

    got = jnp.zeros((8, FMAX), F32)
    for k in range(8):
        hit = (slot == key[k : k + 1]).astype(BF16)
        facts = jnp.where(label == 0, here, jnp.where(label == 1, owner[k : k + 1], 1.0))
        facts = jnp.where(label == 3, float(k), facts)
        got = got + lax.dot_general(
            facts.astype(BF16), hit, (((1,), (1,)), ((), ())), preferred_element_type=F32
        )
    valid = got[2:3]
    index = got[3:4] * float(CZ) + got[0:1]
    who = got[1:2] + valid - 1.0
    zero = jnp.zeros((1, FMAX), F32)
    number = jnp.sum(valid, axis=1, keepdims=True) + zero
    below = [
        jnp.sum(jnp.where(index < at, valid, 0.0), axis=1, keepdims=True) + zero
        for at in (CH // 4, CH // 2, 3 * CH // 4)
    ]
    rows = [index, who, number] + below + [zero, zero]
    lists[...] = jnp.concatenate(rows, axis=0).astype(jnp.int32)


def halo_kernel(
    n_gx, n_gy, fields, diff, reaction, decay, flags, owners,
    cool, hot_out, heat, lists,
    hot, ext, mid, res, ov, taps, matrix, inverse, pad, where, first_t, terms, got, part, back,
    in_sem, send, recv, out_sem, list_sem, hot_sem, heat_send, heat_recv,
):
    gx, gy = lax.axis_index("gx"), lax.axis_index("gy")
    xm, xp = lax.rem(gx + n_gx - 1, n_gx), lax.rem(gx + 1, n_gx)
    ym, yp = lax.rem(gy + n_gy - 1, n_gy), lax.rem(gy + 1, n_gy)
    load = pltpu.make_async_copy(fields, ext.at[:, pl.ds(2, CX), pl.ds(8, CY), :], in_sem)
    load.start()
    targets = [
        (xp, gy), (xm, gy), (gx, yp), (gx, ym), (xp, yp), (xp, ym), (xm, yp), (xm, ym),
    ]
    barrier = pltpu.get_barrier_semaphore()
    for target in targets:
        pl.semaphore_signal(barrier, inc=1, device_id=target, device_id_type=MESH)
    planes = n_gy // 8
    plane = gy // 8
    place = gy - 8 * plane
    near_ones, far_ones = [], []
    for k in range(1, 8):
        other = place + k
        near_ones.append(jnp.where(other >= 8, other - 8, other))
    for k in range(1, planes):
        other = plane + k
        far_ones.append(jnp.where(other >= planes, other - planes, other))
    near_ids = [(gx, plane * 8 + other) for other in near_ones]
    far_ids = [(gx, other * 8 + place) for other in far_ones]
    for target in near_ids + far_ids:
        pl.semaphore_signal(barrier, inc=1, device_id=target, device_id_type=MESH)
    pl.semaphore_wait(barrier, 8 + 7 + planes - 1)
    jobs = []
    for first_c in range(0, COMP, GROUP):
        comps = (first_c, GROUP)
        jobs.append((xp, gy, comps, (CX - 2, 2), (0, CY), (0, 8)))
        jobs.append((xm, gy, comps, (0, 2), (0, CY), (CX + 2, 8)))
    faces = len(jobs)
    every = (0, COMP)
    jobs.append((gx, yp, every, (0, CX), (CY - 2, 2), (2, 6)))
    jobs.append((gx, ym, every, (0, CX), (0, 2), (2, CY + 8)))
    jobs.append((xp, yp, every, (CX - 1, 1), (CY - 1, 1), (1, 7)))
    jobs.append((xp, ym, every, (CX - 1, 1), (0, 1), (1, CY + 8)))
    jobs.append((xm, yp, every, (0, 1), (CY - 1, 1), (CX + 2, 7)))
    jobs.append((xm, ym, every, (0, 1), (0, 1), (CX + 2, CY + 8)))
    copies = []
    for number, (to_x, to_y, comps, xs, ys, (dx, dy)) in enumerate(jobs):
        copies.append(
            pltpu.make_async_remote_copy(
                src_ref=fields.at[pl.ds(*comps), pl.ds(*xs), pl.ds(*ys), :],
                dst_ref=ext.at[pl.ds(*comps), pl.ds(dx, xs[1]), pl.ds(dy, ys[1]), :],
                send_sem=send.at[number],
                recv_sem=recv.at[number],
                device_id=(to_x, to_y),
                device_id_type=MESH,
            )
        )
    for number in list(range(faces, faces + 2)) + list(range(faces)) + list(range(faces + 2, faces + 6)):
        copies[number].start()
    tables(reaction, decay, flags, owners, taps, matrix, inverse, lists, pad)
    listing = pltpu.make_async_copy(lists, where, list_sem)
    listing.start()
    load.wait()

    low_x, high_x = gx == 0, gx == n_gx - 1
    low_y, high_y = gy == 0, gy == n_gy - 1

    def lap(v, near):
        rows = v.shape[0]
        near = near + pltpu.roll(v, 1, 0) + pltpu.roll(v, rows - 1, 0)
        return near + jnp.dot(
            jnp.concatenate(split(v), axis=1), taps[...], preferred_element_type=F32
        )

    def masked(planes):
        top = jnp.where(low_y, 0.0, planes[:, 0:8])
        bottom = jnp.where(high_y, 0.0, planes[:, 8 + CY :])
        return jnp.concatenate([top, planes[:, 8 : 8 + CY], bottom], axis=1)

    def first(c, x, count):
        d = diff[c]
        shape = (count * CY, CZ)

        def rows(at):
            return ext[c, pl.ds(at, count), 8 : 8 + CY].reshape(shape)

        v = rows(x)
        new = v + d * lap(v, rows(x - 1) + rows(x + 1))
        mid[c, pl.ds(x - 1, count), 8 : 8 + CY] = new.reshape(count, CY, CZ)

    def rim(c, x, count):
        d = diff[c]

        def rows(at):
            both = [ext[c, pl.ds(at, count), 0:16], ext[c, pl.ds(at, count), CY : CY + 16]]
            return jnp.concatenate(both, axis=1).reshape(count * 32, CZ)

        v = rows(x)
        new = (v + d * lap(v, rows(x - 1) + rows(x + 1))).reshape(count, 32, CZ)
        to = pl.ds(x - 1, count)
        mid[c, to, 0:8] = jnp.where(low_y, 0.0, new[:, 0:8])
        mid[c, to, 8:9] = new[:, 8:9]
        mid[c, to, CY + 7 : CY + 8] = new[:, 23:24]
        mid[c, to, CY + 8 :] = jnp.where(high_y, 0.0, new[:, 24:32])

    def second(c, x, count):
        d = diff[c]
        shape = (count * 80, CZ)
        v = mid[c, pl.ds(x + 1, count)].reshape(shape)
        near = mid[c, pl.ds(x, count)].reshape(shape) + mid[c, pl.ds(x + 2, count)].reshape(shape)
        new = (v + d * lap(v, near)).reshape(count, 80, CZ)[:, 8 : 8 + CY]
        res[c, pl.ds(x * CY, count * CY)] = new.reshape(count * CY, CZ)

    def outer(cs):
        zero = jnp.zeros((80, CZ), F32)
        centre, near = [], []
        for c in cs:
            a, b, e, f = [ext[c, k] for k in range(4)]
            b = jnp.where(low_x, zero, b)
            centre += [b, e]
            near += [a + e, b + f]
            f, e, b, a = [ext[c, CX + k] for k in range(4)]
            b = jnp.where(high_x, zero, b)
            centre += [e, b]
            near += [f + b, e + a]
        centre = jnp.concatenate(centre, axis=0)
        total = lap(centre, jnp.concatenate(near, axis=0))
        centre2, near2 = [], []
        for k, c in enumerate(cs):
            part = slice(k * 320, k * 320 + 320)
            p = masked((centre[part] + diff[c] * total[part]).reshape(4, 80, CZ))
            m0 = jnp.where(low_x, zero, p[0])
            centre2 += [p[1], mid[c, 2]]
            near2 += [m0 + mid[c, 2], p[1] + mid[c, 3]]
            m1 = jnp.where(high_x, zero, p[3])
            centre2 += [mid[c, CX - 1], p[2]]
            near2 += [mid[c, CX - 2] + p[2], mid[c, CX - 1] + m1]
        centre2 = jnp.concatenate(centre2, axis=0)
        total2 = lap(centre2, jnp.concatenate(near2, axis=0))
        for k, c in enumerate(cs):
            part = slice(k * 320, k * 320 + 320)
            new = (centre2[part] + diff[c] * total2[part]).reshape(4, 80, CZ)[:, 8 : 8 + CY]
            res[c, 0 : 2 * CY] = new[0:2].reshape(2 * CY, CZ)
            res[c, (CX - 2) * CY :] = new[2:4].reshape(2 * CY, CZ)

    def clear(ref, xs, ys):
        @pl.loop(0, COMP)
        def _(c):
            ref[c, pl.ds(*xs), pl.ds(*ys), :] = jnp.zeros((xs[1], ys[1], CZ), F32)

    def edges(ref, xs):
        @pl.when(gy == 0)
        def _():
            clear(ref, xs, (0, 8))

        @pl.when(gy == n_gy - 1)
        def _():
            clear(ref, xs, (CY + 8, 8))

    @pl.loop(0, COMP)
    def _(c):
        first(c, 3, 7)
        first(c, 10, 7)

    copies[faces].wait_recv()
    copies[faces + 1].wait_recv()
    edges(ext, (2, CX))

    @pl.loop(0, COMP)
    def _(c):
        rim(c, 3, 14)

    @pl.loop(0, COMP)
    def _(c):
        second(c, 2, 6)
        second(c, 8, 6)

    inv = inverse[...]
    inv = jnp.concatenate([inv, inv], axis=1)

    def cool_tile(t):
        at = [t * 16 + w * 8 for w in range(2)]
        if not isinstance(t, int):
            at = [pl.multiple_of(a, 8) for a in at]
        groups = [
            jnp.concatenate([res[c, pl.ds(a, 8), :] for c in range(COMP)], axis=0) for a in at
        ]
        rows = substep(jnp.concatenate(groups, axis=1), matrix[...], inv)
        for w in range(2):
            for c in range(COMP):
                ov[c, pl.ds(at[w], 8), :] = rows[c][:, w * CZ : (w + 1) * CZ]

    edge = 2 * CY // 16
    inner = CH // 16 - 2 * edge

    @pl.loop(0, inner // 12)
    def _(k):
        for t in range(12):
            cool_tile(edge + k * 12 + t)

    def store(k, start, size):
        where_to = pl.ds(start, size)
        return pltpu.make_async_copy(ov.at[:, where_to, :], cool.at[:, where_to, :], out_sem.at[k])

    stores = [
        store(0, 2 * CY, (CX - 4) * CY), store(1, 0, 2 * CY), store(2, (CX - 2) * CY, 2 * CY),
    ]
    stores[0].start()

    for number in range(faces + 2, faces + 6):
        copies[number].wait_recv()
    edges(ext, (1, 1))
    edges(ext, (CX + 2, 1))

    for group in range(faces // 2):
        copies[2 * group].wait_recv()
        copies[2 * group + 1].wait_recv()
        cs = list(range(group * GROUP, (group + 1) * GROUP))
        outer(cs)

    listing.wait()

    @pl.loop(0, FMAX // 8)
    def _(g):
        for r in range(8):
            at = jnp.clip(where[0, g * 8 + r], 0, CH - 1)
            for c in range(COMP):
                hot[g, pl.ds(c * 8 + r, 1), :] = res[c, pl.ds(at, 1), :]
        first_t[g] = hot[g, 72:80, :]

    @pl.loop(0, FLAME_SUB)
    def _(s):
        for t in range(FMAX // 16):
            flame_tile(hot, t, matrix, inv)

    leaving = pltpu.make_async_copy(hot, hot_out, hot_sem)
    leaving.start()
    gain = (hot[:, 72:80, :] - first_t[...]).reshape(FMAX, CZ)
    row = lax.broadcasted_iota(jnp.int32, (64, FMAX), 0)
    owner = jnp.where((row & 7) < planes, (row & 7) * 8 + (row >> 3), -2)
    onehot = (owner == lists[1:2, :]).astype(BF16)
    total = jnp.zeros((64, CZ), F32)
    for piece in split(gain):
        total = total + jnp.dot(onehot, piece, preferred_element_type=F32)
    terms[...] = total.reshape(8, 8, CZ)

    sums = []
    for k, (other, target) in enumerate(zip(near_ones, near_ids)):
        copy = pltpu.make_async_remote_copy(
            src_ref=terms.at[other],
            dst_ref=got.at[k],
            send_sem=heat_send.at[k],
            recv_sem=heat_recv.at[k],
            device_id=target,
            device_id_type=MESH,
        )
        copy.start()
        sums.append(copy)
    for t in range(edge):
        cool_tile(t)
    stores[1].start()
    total = terms[place]
    for k in range(7):
        sums[k].wait_recv()
        total = total + got[k]
    part[...] = total
    for k, target in enumerate(far_ids):
        copy = pltpu.make_async_remote_copy(
            src_ref=part,
            dst_ref=back.at[k],
            send_sem=heat_send.at[7 + k],
            recv_sem=heat_recv.at[7 + k],
            device_id=target,
            device_id_type=MESH,
        )
        copy.start()
        sums.append(copy)
    for t in range(edge):
        cool_tile(edge + inner + t)
    stores[2].start()
    for k in range(planes - 1):
        sums[7 + k].wait_recv()
        total = total + back[k]
    total = jnp.where(lax.broadcasted_iota(jnp.int32, (8, CZ), 0) == plane, total, 0.0)
    total = jnp.sum(jnp.sum(total, axis=0, keepdims=True), axis=1, keepdims=True)
    heat[...] = total * (1.0 / math.sqrt(CZ) / math.sqrt(RMAX))
    for copy in copies + sums:
        copy.wait_send()
    leaving.wait()
    for copy in stores:
        copy.wait()


def sigmoid(x):
    return 0.5 * jnp.tanh(0.5 * x) + 0.5


def substep(state, matrix, inverse):
    high, low = split(state)
    r = jnp.dot(matrix, jnp.concatenate([high, low, high], axis=0), preferred_element_type=F32)
    last = state[72:80]
    base = last * inverse[72:80]
    g0 = sigmoid(last)
    g1 = sigmoid(base + g0 * r[240:248])
    g2 = sigmoid(base + g1 * (r[72:80] + g0 * r[248:256]))
    rows = []
    for c in range(COMP):
        at = 8 * c
        inner = r[80 + at : 88 + at] + g0 * r[160 + at : 168 + at]
        rows.append(state[at : at + 8] * inverse[at : at + 8] + g2 * (r[at : at + 8] + g1 * inner))
    return rows


def flame_tile(cur, t, matrix, inv):
    rows = substep(jnp.concatenate([cur[2 * t], cur[2 * t + 1]], axis=1), matrix[...], inv)
    new = jnp.concatenate(rows, axis=0)
    cur[2 * t] = new[:, :CZ]
    cur[2 * t + 1] = new[:, CZ:]


def merge_kernel(cool, hot_in, index, out, ov, hot, in_sem, hot_sem, out_sem):
    quarter = CH // 4

    def fetch(k):
        at = pl.ds(k * quarter, quarter)
        return pltpu.make_async_copy(cool.at[:, at, :], ov.at[:, at, :], in_sem.at[k])

    def flush(k):
        at = pl.ds(k * quarter, quarter)
        return pltpu.make_async_copy(ov.at[:, at, :], out.at[:, at, :], out_sem.at[k])

    flames = pltpu.make_async_copy(hot_in, hot, hot_sem)
    fetch(0).start()
    flames.start()
    for k in range(1, 4):
        fetch(k).start()
    flames.wait()
    start = 0
    for k in range(4):
        stop = jnp.clip(index[3 + k, 0] if k < 3 else index[2, 0], 0, FMAX)
        fetch(k).wait()

        @pl.loop(0, (jnp.maximum(stop - start, 0) + 7) // 8)
        def _(g, start=start, stop=stop):
            for r in range(8):
                p = jnp.minimum(start + g * 8 + r, stop - 1)
                at = index[0, p]
                for c in range(COMP):
                    ov[c, pl.ds(at, 1), :] = hot[p >> 3, pl.ds(c * 8 + (p & 7), 1), :]

        start = stop
        flush(k).start()
    for k in range(4):
        flush(k).wait()


def per_device(n_gx, n_gy, fields, diffusivity, decay_rates, reaction_matrix, owner_index, flame_flag):
    shape = (COMP, CH, CZ)
    groups = FMAX // 8
    faces = 2 * (COMP // GROUP)
    partners = 7 + n_gy // 8 - 1
    dma = pltpu.SemaphoreType.DMA
    as_f32 = lambda *dims: jax.ShapeDtypeStruct(dims, F32)
    cool, hot, heat, lists = pl.pallas_call(
        functools.partial(halo_kernel, n_gx, n_gy),
        out_shape=(
            as_f32(*shape),
            as_f32(groups, 80, CZ),
            as_f32(1, 1),
            jax.ShapeDtypeStruct((8, FMAX), jnp.int32),
        ),
        in_specs=[ANY, SMEM, VMEM, SMEM, VMEM, VMEM],
        out_specs=(ANY, ANY, VMEM, VMEM),
        scratch_shapes=[
            pltpu.VMEM((groups, 80, CZ), F32),
            pltpu.VMEM((COMP, CX + 4, CY + 16, CZ), F32),
            pltpu.VMEM((COMP, CX + 2, CY + 16, CZ), F32),
            pltpu.VMEM(shape, F32),
            pltpu.VMEM(shape, F32),
            pltpu.VMEM((2 * CZ, CZ), BF16),
            pltpu.VMEM((256, 240), BF16),
            pltpu.VMEM((80, CZ), F32),
            pltpu.VMEM((CZ, CZ), F32),
            pltpu.SMEM((8, FMAX), jnp.int32),
            pltpu.VMEM((groups, 8, CZ), F32),
            pltpu.VMEM((8, 8, CZ), F32),
            pltpu.VMEM((7, 8, CZ), F32),
            pltpu.VMEM((8, CZ), F32),
            pltpu.VMEM((n_gy // 8 - 1, 8, CZ), F32),
            dma,
            dma((faces + 6,)),
            dma((faces + 6,)),
            dma((3,)),
            dma,
            dma,
            dma((partners,)),
            dma((partners,)),
        ],
        compiler_params=pltpu.CompilerParams(
            collective_id=0, has_side_effects=True, vmem_limit_bytes=LIMIT
        ),
        name="halo_diffuse_react",
    )(
        fields, diffusivity, reaction_matrix, decay_rates,
        flame_flag.reshape(8, CZ), owner_index.reshape(8, CZ),
    )
    merged = pl.pallas_call(
        merge_kernel,
        out_shape=as_f32(*shape),
        in_specs=[ANY, ANY, SMEM],
        out_specs=ANY,
        scratch_shapes=[
            pltpu.VMEM(shape, F32),
            pltpu.VMEM((groups, 80, CZ), F32),
            dma((4,)),
            dma,
            dma((4,)),
        ],
        compiler_params=pltpu.CompilerParams(vmem_limit_bytes=LIMIT),
        name="merge_flames",
    )(cool, hot, lists)
    return merged.reshape(COMP, CX, CY, CZ), heat


def solution(mesh):
    return jax.shard_map(
        functools.partial(per_device, mesh.shape["gx"], mesh.shape["gy"]),
        mesh=mesh,
        in_specs=(
            P(None, "gx", "gy", None),
            P(),
            P(),
            P(),
            P("gx", "gy", None),
            P("gx", "gy", None),
        ),
        out_specs=(P(None, "gx", "gy", None), P("gx", "gy")),
        check_vma=False,
    )
```

```python
import functools
import math

import jax
import jax.numpy as jnp
from jax import lax
from jax.experimental import pallas as pl
from jax.experimental.pallas import tpu as pltpu
from jax.sharding import PartitionSpec as P

H_STEP = 0.2
FLAME_SUB = 10
COMP = 10
CX, CY, CZ = 16, 64, 128
CH = CX * CY
FMAX = 256
RMAX = 60
GROUP = 5

F32, BF16 = jnp.float32, jnp.bfloat16
MESH = pl.DeviceIdType.MESH
VMEM = pl.BlockSpec(memory_space=pltpu.VMEM)
SMEM = pl.BlockSpec(memory_space=pltpu.SMEM)
ANY = pl.BlockSpec(memory_space=pl.ANY)
LIMIT = 56 << 20


def split(values):
    high = values.astype(BF16)
    low = (values - high.astype(F32)).astype(BF16)
    return high, low


def tables(reaction, decay, flags, owners, taps, matrix, inverse, lists, pad):
    exact = lax.Precision.HIGHEST
    iota = lax.broadcasted_iota
    one = jnp.float32(1.0)
    gap = jnp.abs((iota(jnp.int32, (2 * CZ, CZ), 0) & (CZ - 1)) - iota(jnp.int32, (2 * CZ, CZ), 1))
    taps[...] = jnp.where(gap == 0, -6.0, jnp.where(gap == 1, 1.0, 0.0)).astype(BF16)

    shares = [one / (one + H_STEP * jnp.full((8, CZ), decay[c], F32)) for c in range(COMP)]
    for c in range(COMP):
        inverse[pl.ds(8 * c, 8), :] = shares[c]
    sub, lane = iota(jnp.int32, (16, CZ), 0), iota(jnp.int32, (16, CZ), 1)
    by_row = jnp.zeros((16, CZ), F32)
    by_lane = jnp.zeros((16, CZ), F32)
    for c in range(COMP):
        share = jnp.concatenate([shares[c], shares[c]], axis=0)
        by_row = jnp.where(sub == c, share, by_row)
        by_lane = jnp.where(lane == c, share, by_lane)
    pad[...] = jnp.zeros((CZ, CZ), F32)
    pad[0:COMP, 0:COMP] = reaction[...]
    m1 = H_STEP * pad[0:16, :] * by_row
    pad[0:16, :] = m1
    full = pad[...]
    m2 = jnp.dot(m1, full, precision=exact, preferred_element_type=F32)
    m3 = jnp.dot(m2, full, precision=exact, preferred_element_type=F32)
    d1, d2 = m1 * by_lane, m2 * by_lane
    every = jnp.concatenate([d1, d2, m3, m1, m2], axis=0)
    high, low = split(every)
    row = iota(jnp.int32, (256, 80), 0) >> 3
    source = row + 6 * (row >= 10).astype(jnp.int32) + 6 * (row >= 20).astype(jnp.int32)
    source = jnp.where(row == 30, 48 + 9, jnp.where(row == 31, 64 + 9, source))
    up = (source == iota(jnp.int32, (256, 80), 1)).astype(BF16)
    column = iota(jnp.int32, (CZ, 240), 1)
    third = (column >= 80).astype(jnp.int32) + (column >= 160).astype(jnp.int32)
    across = (((column - 80 * third) >> 3) == iota(jnp.int32, (CZ, 240), 0)).astype(BF16)
    spread = [
        jnp.dot(
            jnp.dot(up, part, preferred_element_type=F32).astype(BF16),
            across,
            preferred_element_type=F32,
        )
        for part in (high, low)
    ]
    r, n = iota(jnp.int32, (256, 240), 0), iota(jnp.int32, (256, 240), 1)
    value = jnp.where(n < 160, spread[0], spread[1])
    matrix[...] = jnp.where((r & 7) == (n & 7), value, 0.0).astype(BF16)

    flame = flags[...].astype(F32)
    upper = (iota(jnp.int32, (CZ, CZ), 0) <= iota(jnp.int32, (CZ, CZ), 1)).astype(BF16)
    count = jnp.dot(flame.astype(BF16), upper, preferred_element_type=F32)
    total = jnp.dot(flame.astype(BF16), jnp.ones((CZ, CZ), BF16), preferred_element_type=F32)
    before = jnp.zeros((1, CZ), F32)
    keys = []
    for k in range(8):
        keys.append(count[k : k + 1] - 1.0 + before)
        before = before + total[k : k + 1]
    key = jnp.where(flame > 0.0, jnp.concatenate(keys, axis=0), -1.0)
    slot = iota(jnp.int32, (FMAX, CZ), 0).astype(F32)
    label = iota(jnp.int32, (8, CZ), 0)
    here = iota(jnp.int32, (8, CZ), 1).astype(F32)
    owner = owners[...].astype(F32)

    got = jnp.zeros((8, FMAX), F32)
    for k in range(8):
        hit = (slot == key[k : k + 1]).astype(BF16)
        facts = jnp.where(label == 0, here, jnp.where(label == 1, owner[k : k + 1], 1.0))
        facts = jnp.where(label == 3, float(k), facts)
        got = got + lax.dot_general(
            facts.astype(BF16), hit, (((1,), (1,)), ((), ())), preferred_element_type=F32
        )
    valid = got[2:3]
    index = got[3:4] * float(CZ) + got[0:1]
    who = got[1:2] + valid - 1.0
    zero = jnp.zeros((1, FMAX), F32)
    number = jnp.sum(valid, axis=1, keepdims=True) + zero
    below = [
        jnp.sum(jnp.where(index < at, valid, 0.0), axis=1, keepdims=True) + zero
        for at in (CH // 4, CH // 2, 3 * CH // 4)
    ]
    rows = [index, who, number] + below + [zero, zero]
    lists[...] = jnp.concatenate(rows, axis=0).astype(jnp.int32)


def halo_kernel(
    n_gx, n_gy, fields, diff, reaction, decay, flags, owners,
    cool, hot_out, heat, lists,
    hot, ext, mid, res, ov, taps, matrix, inverse, pad, where, first_t, terms, got, part, back,
    in_sem, send, recv, out_sem, list_sem, hot_sem, heat_send, heat_recv,
):
    gx, gy = lax.axis_index("gx"), lax.axis_index("gy")
    xm, xp = lax.rem(gx + n_gx - 1, n_gx), lax.rem(gx + 1, n_gx)
    ym, yp = lax.rem(gy + n_gy - 1, n_gy), lax.rem(gy + 1, n_gy)
    load = pltpu.make_async_copy(fields, ext.at[:, pl.ds(2, CX), pl.ds(8, CY), :], in_sem)
    load.start()
    targets = [
        (xp, gy), (xm, gy), (gx, yp), (gx, ym), (xp, yp), (xp, ym), (xm, yp), (xm, ym),
    ]
    barrier = pltpu.get_barrier_semaphore()
    for target in targets:
        pl.semaphore_signal(barrier, inc=1, device_id=target, device_id_type=MESH)
    planes = n_gy // 8
    plane = gy // 8
    place = gy - 8 * plane
    near_ones, far_ones = [], []
    for k in range(1, 8):
        other = place + k
        near_ones.append(jnp.where(other >= 8, other - 8, other))
    for k in range(1, planes):
        other = plane + k
        far_ones.append(jnp.where(other >= planes, other - planes, other))
    near_ids = [(gx, plane * 8 + other) for other in near_ones]
    far_ids = [(gx, other * 8 + place) for other in far_ones]
    for target in near_ids + far_ids:
        pl.semaphore_signal(barrier, inc=1, device_id=target, device_id_type=MESH)
    pl.semaphore_wait(barrier, 8 + 7 + planes - 1)
    jobs = []
    for first_c in range(0, COMP, GROUP):
        comps = (first_c, GROUP)
        jobs.append((xp, gy, comps, (CX - 2, 2), (0, CY), (0, 8)))
        jobs.append((xm, gy, comps, (0, 2), (0, CY), (CX + 2, 8)))
    faces = len(jobs)
    every = (0, COMP)
    jobs.append((gx, yp, every, (0, CX), (CY - 2, 2), (2, 6)))
    jobs.append((gx, ym, every, (0, CX), (0, 2), (2, CY + 8)))
    jobs.append((xp, yp, every, (CX - 1, 1), (CY - 1, 1), (1, 7)))
    jobs.append((xp, ym, every, (CX - 1, 1), (0, 1), (1, CY + 8)))
    jobs.append((xm, yp, every, (0, 1), (CY - 1, 1), (CX + 2, 7)))
    jobs.append((xm, ym, every, (0, 1), (0, 1), (CX + 2, CY + 8)))
    copies = []
    for number, (to_x, to_y, comps, xs, ys, (dx, dy)) in enumerate(jobs):
        copies.append(
            pltpu.make_async_remote_copy(
                src_ref=fields.at[pl.ds(*comps), pl.ds(*xs), pl.ds(*ys), :],
                dst_ref=ext.at[pl.ds(*comps), pl.ds(dx, xs[1]), pl.ds(dy, ys[1]), :],
                send_sem=send.at[number],
                recv_sem=recv.at[number],
                device_id=(to_x, to_y),
                device_id_type=MESH,
            )
        )
    for number in list(range(faces, faces + 2)) + list(range(faces)) + list(range(faces + 2, faces + 6)):
        copies[number].start()
    tables(reaction, decay, flags, owners, taps, matrix, inverse, lists, pad)
    listing = pltpu.make_async_copy(lists, where, list_sem)
    listing.start()
    load.wait()

    low_x, high_x = gx == 0, gx == n_gx - 1
    low_y, high_y = gy == 0, gy == n_gy - 1

    def lap(v, near):
        rows = v.shape[0]
        near = near + pltpu.roll(v, 1, 0) + pltpu.roll(v, rows - 1, 0)
        return near + jnp.dot(
            jnp.concatenate(split(v), axis=1), taps[...], preferred_element_type=F32
        )

    def masked(planes):
        top = jnp.where(low_y, 0.0, planes[:, 0:8])
        bottom = jnp.where(high_y, 0.0, planes[:, 8 + CY :])
        return jnp.concatenate([top, planes[:, 8 : 8 + CY], bottom], axis=1)

    def first(c, x, count):
        d = diff[c]
        shape = (count * CY, CZ)

        def rows(at):
            return ext[c, pl.ds(at, count), 8 : 8 + CY].reshape(shape)

        v = rows(x)
        new = v + d * lap(v, rows(x - 1) + rows(x + 1))
        mid[c, pl.ds(x - 1, count), 8 : 8 + CY] = new.reshape(count, CY, CZ)

    def rim(c, x, count):
        d = diff[c]

        def rows(at):
            both = [ext[c, pl.ds(at, count), 0:16], ext[c, pl.ds(at, count), CY : CY + 16]]
            return jnp.concatenate(both, axis=1).reshape(count * 32, CZ)

        v = rows(x)
        new = (v + d * lap(v, rows(x - 1) + rows(x + 1))).reshape(count, 32, CZ)
        to = pl.ds(x - 1, count)
        mid[c, to, 0:8] = jnp.where(low_y, 0.0, new[:, 0:8])
        mid[c, to, 8:9] = new[:, 8:9]
        mid[c, to, CY + 7 : CY + 8] = new[:, 23:24]
        mid[c, to, CY + 8 :] = jnp.where(high_y, 0.0, new[:, 24:32])

    def second(c, x, count):
        d = diff[c]
        shape = (count * 80, CZ)
        v = mid[c, pl.ds(x + 1, count)].reshape(shape)
        near = mid[c, pl.ds(x, count)].reshape(shape) + mid[c, pl.ds(x + 2, count)].reshape(shape)
        new = (v + d * lap(v, near)).reshape(count, 80, CZ)[:, 8 : 8 + CY]
        res[c, pl.ds(x * CY, count * CY)] = new.reshape(count * CY, CZ)

    def outer(cs):
        zero = jnp.zeros((80, CZ), F32)
        centre, near = [], []
        for c in cs:
            a, b, e, f = [ext[c, k] for k in range(4)]
            b = jnp.where(low_x, zero, b)
            centre += [b, e]
            near += [a + e, b + f]
            f, e, b, a = [ext[c, CX + k] for k in range(4)]
            b = jnp.where(high_x, zero, b)
            centre += [e, b]
            near += [f + b, e + a]
        centre = jnp.concatenate(centre, axis=0)
        total = lap(centre, jnp.concatenate(near, axis=0))
        centre2, near2 = [], []
        for k, c in enumerate(cs):
            part = slice(k * 320, k * 320 + 320)
            p = masked((centre[part] + diff[c] * total[part]).reshape(4, 80, CZ))
            m0 = jnp.where(low_x, zero, p[0])
            centre2 += [p[1], mid[c, 2]]
            near2 += [m0 + mid[c, 2], p[1] + mid[c, 3]]
            m1 = jnp.where(high_x, zero, p[3])
            centre2 += [mid[c, CX - 1], p[2]]
            near2 += [mid[c, CX - 2] + p[2], mid[c, CX - 1] + m1]
        centre2 = jnp.concatenate(centre2, axis=0)
        total2 = lap(centre2, jnp.concatenate(near2, axis=0))
        for k, c in enumerate(cs):
            part = slice(k * 320, k * 320 + 320)
            new = (centre2[part] + diff[c] * total2[part]).reshape(4, 80, CZ)[:, 8 : 8 + CY]
            res[c, 0 : 2 * CY] = new[0:2].reshape(2 * CY, CZ)
            res[c, (CX - 2) * CY :] = new[2:4].reshape(2 * CY, CZ)

    def clear(ref, xs, ys):
        @pl.loop(0, COMP)
        def _(c):
            ref[c, pl.ds(*xs), pl.ds(*ys), :] = jnp.zeros((xs[1], ys[1], CZ), F32)

    def edges(ref, xs):
        @pl.when(gy == 0)
        def _():
            clear(ref, xs, (0, 8))

        @pl.when(gy == n_gy - 1)
        def _():
            clear(ref, xs, (CY + 8, 8))

    @pl.loop(0, COMP)
    def _(c):
        first(c, 3, 7)
        first(c, 10, 7)

    copies[faces].wait_recv()
    copies[faces + 1].wait_recv()
    edges(ext, (2, CX))

    @pl.loop(0, COMP)
    def _(c):
        rim(c, 3, 14)

    @pl.loop(0, COMP)
    def _(c):
        second(c, 2, 6)
        second(c, 8, 6)

    inv = inverse[...]
    inv = jnp.concatenate([inv, inv], axis=1)

    def cool_tile(t):
        at = [t * 16 + w * 8 for w in range(2)]
        if not isinstance(t, int):
            at = [pl.multiple_of(a, 8) for a in at]
        groups = [
            jnp.concatenate([res[c, pl.ds(a, 8), :] for c in range(COMP)], axis=0) for a in at
        ]
        rows = substep(jnp.concatenate(groups, axis=1), matrix[...], inv)
        for w in range(2):
            for c in range(COMP):
                ov[c, pl.ds(at[w], 8), :] = rows[c][:, w * CZ : (w + 1) * CZ]

    edge = 2 * CY // 16
    inner = CH // 16 - 2 * edge

    @pl.loop(0, inner // 12)
    def _(k):
        for t in range(12):
            cool_tile(edge + k * 12 + t)

    def store(k, start, size):
        where_to = pl.ds(start, size)
        return pltpu.make_async_copy(ov.at[:, where_to, :], cool.at[:, where_to, :], out_sem.at[k])

    stores = [
        store(0, 2 * CY, (CX - 4) * CY), store(1, 0, 2 * CY), store(2, (CX - 2) * CY, 2 * CY),
    ]
    stores[0].start()

    for number in range(faces + 2, faces + 6):
        copies[number].wait_recv()
    edges(ext, (1, 1))
    edges(ext, (CX + 2, 1))

    for group in range(faces // 2):
        copies[2 * group].wait_recv()
        copies[2 * group + 1].wait_recv()
        cs = list(range(group * GROUP, (group + 1) * GROUP))
        outer(cs)

    listing.wait()

    @pl.loop(0, FMAX // 8)
    def _(g):
        for r in range(8):
            at = jnp.clip(where[0, g * 8 + r], 0, CH - 1)
            for c in range(COMP):
                hot[g, pl.ds(c * 8 + r, 1), :] = res[c, pl.ds(at, 1), :]
        first_t[g] = hot[g, 72:80, :]

    @pl.loop(0, FLAME_SUB // 2)
    def _(s):
        for t in list(range(FMAX // 16)) * 2:
            flame_tile(hot, t, matrix, inv)

    leaving = pltpu.make_async_copy(hot, hot_out, hot_sem)
    leaving.start()
    gain = (hot[:, 72:80, :] - first_t[...]).reshape(FMAX, CZ)
    row = lax.broadcasted_iota(jnp.int32, (64, FMAX), 0)
    owner = jnp.where((row & 7) < planes, (row & 7) * 8 + (row >> 3), -2)
    onehot = (owner == lists[1:2, :]).astype(BF16)
    total = jnp.zeros((64, CZ), F32)
    for piece in split(gain):
        total = total + jnp.dot(onehot, piece, preferred_element_type=F32)
    terms[...] = total.reshape(8, 8, CZ)

    sums = []
    for k, (other, target) in enumerate(zip(near_ones, near_ids)):
        copy = pltpu.make_async_remote_copy(
            src_ref=terms.at[other],
            dst_ref=got.at[k],
            send_sem=heat_send.at[k],
            recv_sem=heat_recv.at[k],
            device_id=target,
            device_id_type=MESH,
        )
        copy.start()
        sums.append(copy)
    for t in range(edge):
        cool_tile(t)
    stores[1].start()
    total = terms[place]
    for k in range(7):
        sums[k].wait_recv()
        total = total + got[k]
    part[...] = total
    for k, target in enumerate(far_ids):
        copy = pltpu.make_async_remote_copy(
            src_ref=part,
            dst_ref=back.at[k],
            send_sem=heat_send.at[7 + k],
            recv_sem=heat_recv.at[7 + k],
            device_id=target,
            device_id_type=MESH,
        )
        copy.start()
        sums.append(copy)
    for t in range(edge):
        cool_tile(edge + inner + t)
    stores[2].start()
    for k in range(planes - 1):
        sums[7 + k].wait_recv()
        total = total + back[k]
    total = jnp.where(lax.broadcasted_iota(jnp.int32, (8, CZ), 0) == plane, total, 0.0)
    total = jnp.sum(jnp.sum(total, axis=0, keepdims=True), axis=1, keepdims=True)
    heat[...] = total * (1.0 / math.sqrt(CZ) / math.sqrt(RMAX))
    for copy in copies + sums:
        copy.wait_send()
    leaving.wait()
    for copy in stores:
        copy.wait()


def sigmoid(x):
    return 0.5 * jnp.tanh(0.5 * x) + 0.5


def substep(state, matrix, inverse):
    high, low = split(state)
    r = jnp.dot(matrix, jnp.concatenate([high, low, high], axis=0), preferred_element_type=F32)
    last = state[72:80]
    base = last * inverse[72:80]
    g0 = sigmoid(last)
    g1 = sigmoid(base + g0 * r[240:248])
    g2 = sigmoid(base + g1 * (r[72:80] + g0 * r[248:256]))
    rows = []
    for c in range(COMP):
        at = 8 * c
        inner = r[80 + at : 88 + at] + g0 * r[160 + at : 168 + at]
        rows.append(state[at : at + 8] * inverse[at : at + 8] + g2 * (r[at : at + 8] + g1 * inner))
    return rows


def flame_tile(cur, t, matrix, inv):
    rows = substep(jnp.concatenate([cur[2 * t], cur[2 * t + 1]], axis=1), matrix[...], inv)
    new = jnp.concatenate(rows, axis=0)
    cur[2 * t] = new[:, :CZ]
    cur[2 * t + 1] = new[:, CZ:]


def merge_kernel(cool, hot_in, index, out, ov, hot, in_sem, hot_sem, out_sem):
    quarter = CH // 4

    def fetch(k):
        at = pl.ds(k * quarter, quarter)
        return pltpu.make_async_copy(cool.at[:, at, :], ov.at[:, at, :], in_sem.at[k])

    def flush(k):
        at = pl.ds(k * quarter, quarter)
        return pltpu.make_async_copy(ov.at[:, at, :], out.at[:, at, :], out_sem.at[k])

    flames = pltpu.make_async_copy(hot_in, hot, hot_sem)
    fetch(0).start()
    flames.start()
    for k in range(1, 4):
        fetch(k).start()
    flames.wait()
    start = 0
    for k in range(4):
        stop = jnp.clip(index[3 + k, 0] if k < 3 else index[2, 0], 0, FMAX)
        fetch(k).wait()

        @pl.loop(0, (jnp.maximum(stop - start, 0) + 7) // 8)
        def _(g, start=start, stop=stop):
            for r in range(8):
                p = jnp.minimum(start + g * 8 + r, stop - 1)
                at = index[0, p]
                for c in range(COMP):
                    ov[c, pl.ds(at, 1), :] = hot[p >> 3, pl.ds(c * 8 + (p & 7), 1), :]

        start = stop
        flush(k).start()
    for k in range(4):
        flush(k).wait()


def per_device(n_gx, n_gy, fields, diffusivity, decay_rates, reaction_matrix, owner_index, flame_flag):
    shape = (COMP, CH, CZ)
    groups = FMAX // 8
    faces = 2 * (COMP // GROUP)
    partners = 7 + n_gy // 8 - 1
    dma = pltpu.SemaphoreType.DMA
    as_f32 = lambda *dims: jax.ShapeDtypeStruct(dims, F32)
    cool, hot, heat, lists = pl.pallas_call(
        functools.partial(halo_kernel, n_gx, n_gy),
        out_shape=(
            as_f32(*shape),
            as_f32(groups, 80, CZ),
            as_f32(1, 1),
            jax.ShapeDtypeStruct((8, FMAX), jnp.int32),
        ),
        in_specs=[ANY, SMEM, VMEM, SMEM, VMEM, VMEM],
        out_specs=(ANY, ANY, VMEM, VMEM),
        scratch_shapes=[
            pltpu.VMEM((groups, 80, CZ), F32),
            pltpu.VMEM((COMP, CX + 4, CY + 16, CZ), F32),
            pltpu.VMEM((COMP, CX + 2, CY + 16, CZ), F32),
            pltpu.VMEM(shape, F32),
            pltpu.VMEM(shape, F32),
            pltpu.VMEM((2 * CZ, CZ), BF16),
            pltpu.VMEM((256, 240), BF16),
            pltpu.VMEM((80, CZ), F32),
            pltpu.VMEM((CZ, CZ), F32),
            pltpu.SMEM((8, FMAX), jnp.int32),
            pltpu.VMEM((groups, 8, CZ), F32),
            pltpu.VMEM((8, 8, CZ), F32),
            pltpu.VMEM((7, 8, CZ), F32),
            pltpu.VMEM((8, CZ), F32),
            pltpu.VMEM((n_gy // 8 - 1, 8, CZ), F32),
            dma,
            dma((faces + 6,)),
            dma((faces + 6,)),
            dma((3,)),
            dma,
            dma,
            dma((partners,)),
            dma((partners,)),
        ],
        compiler_params=pltpu.CompilerParams(
            collective_id=0, has_side_effects=True, vmem_limit_bytes=LIMIT
        ),
        name="halo_diffuse_react",
    )(
        fields, diffusivity, reaction_matrix, decay_rates,
        flame_flag.reshape(8, CZ), owner_index.reshape(8, CZ),
    )
    merged = pl.pallas_call(
        merge_kernel,
        out_shape=as_f32(*shape),
        in_specs=[ANY, ANY, SMEM],
        out_specs=ANY,
        scratch_shapes=[
            pltpu.VMEM(shape, F32),
            pltpu.VMEM((groups, 80, CZ), F32),
            dma((4,)),
            dma,
            dma((4,)),
        ],
        compiler_params=pltpu.CompilerParams(vmem_limit_bytes=LIMIT),
        name="merge_flames",
    )(cool, hot, lists)
    return merged.reshape(COMP, CX, CY, CZ), heat


def solution(mesh):
    return jax.shard_map(
        functools.partial(per_device, mesh.shape["gx"], mesh.shape["gy"]),
        mesh=mesh,
        in_specs=(
            P(None, "gx", "gy", None),
            P(),
            P(),
            P(),
            P("gx", "gy", None),
            P("gx", "gy", None),
        ),
        out_specs=(P(None, "gx", "gy", None), P("gx", "gy")),
        check_vma=False,
    )
```
